32 devices in a mesh: section: 4 (over y, core), dp: 8 (over z, x).
Axes of the slice: x: 2, y: 2, z: 4, core: 2. Of those that a mesh axis runs over, the one named last changes fastest.
Arguments:
- latents: bfloat16 [6, 176, 1536], P(None, 'dp'), may hold values from -6 to 6
- control_hint: bfloat16 [6, 176, 1536], P(None, 'dp'), may hold values from -6 to 6
- upstream: bfloat16 [6, 176, 1536], P(None, 'dp'), may hold values from -6 to 6
- batch_order: int32 [6], replicated, may hold values from 0 to 5, each once
- section_weight: bfloat16 [4, 1536, 1536], P('section'), may hold values from -0.078125 to 0.078125
- zero_weight: bfloat16 [4, 768, 1536], P('section'), may hold values from -0.0390625 to 0.0390625
Outputs:
- zero_grad: float32 [4, 768, 1536], P('section', 'dp')
The draws below stay inside these ranges and needn't reach their ends.
Inputs may be any that keep to these rules, and one draw needn't show every extreme that they name: batch_order names each of the 6 micro-batches exactly once.
All inputs are finite; a program needn't handle non-finite values.
Results may differ from the reference program's by a relative error of at most 0.03.
Values may be sent and summed in bfloat16 or wider, within the bound.
A program may use at most 64 MiB of HBM per device.

```python
import math
import jax
import jax.numpy as jnp
from jax import lax

D = 1536
MICRO = 6
ROWS = 22
TOKENS = 176
HALF = 768
N_SECTION = 4
N_DP = 8


def spiked(result, own_key, source, target, shards_of, factor):
    owner, partner = [(jnp.arange(result.shape[position]) // (result.shape[position] // shards_of)).reshape([-1 if axis == position else 1 for axis in range(result.ndim)]) for position in (source, target)]
    chosen = jax.random.permutation(own_key, shards_of)[partner]
    strong = (owner == chosen) | (owner == (partner + shards_of // 2) % shards_of)
    return jnp.where(strong, factor * result, result)


def steps_of(key, extent, cuts, smallest, top_value):
    level, own = 1.0, jax.random.fold_in(key, 6)
    for dim, blocks in cuts:
        steps = jnp.exp(jax.random.uniform(jax.random.fold_in(own, dim), (blocks,), jnp.float32, smallest / len(cuts), top_value / len(cuts)))
        level = level * jnp.repeat(steps, extent[dim] // blocks).reshape([-1 if axis == dim else 1 for axis in range(len(extent))])
    return level


def bell_draw(stream_key, dims, deviation, bound, shards=(), kind=jnp.bfloat16):
    values = jax.random.normal(stream_key, dims, jnp.float32) * deviation
    if len(shards) > 0:
        values = steps_of(stream_key, dims, shards, -0.22, 0.18) * values
    return jnp.clip(values, min=-bound, max=bound).astype(kind)


def gaussian_with(key, extent, scale, reach, shards, heavy, dtype=jnp.bfloat16):
    values = scale * jax.random.normal(key, extent, jnp.float32)
    if shards:
        values = values * steps_of(key, extent, shards, -0.22, 0.18)
    return jnp.clip(spiked(values, jax.random.fold_in(key, 3), *heavy), -reach, reach).astype(dtype)


def setup_inputs(seed: int = 0) -> dict:
    splits = jax.random.split(jax.random.key(seed), 7)
    return {
        "latents": bell_draw(splits[0], (MICRO, TOKENS, D), 1.0, 6.0, ((1, 8),)),
        "control_hint": gaussian_with(splits[1], (MICRO, TOKENS, D), 1.0, 6.0, ((1, 8),), (1, 2, 8, 2.0)),
        "upstream": bell_draw(splits[2], (MICRO, TOKENS, D), 1.0, 6.0, ((1, 8),)),
        "batch_order": jax.random.permutation(splits[3], MICRO).astype(jnp.int32),
        "section_weight": bell_draw(splits[4], (N_SECTION, D, D), (4 * D) ** -0.5, 0.078125, ((0, 4),)),
        "zero_weight": bell_draw(splits[5], (N_SECTION, HALF, D), (16 * D) ** -0.5, 0.0390625, ((0, 4),)),
    }


tanh_coef = 0.7978845608028654
cube_coef = 0.044715

def gelu_value(values):
    inner = tanh_coef * (values + cube_coef * values * values * values)
    return 0.5 * values * (1.0 + jnp.tanh(inner))

def gelu_slope(values):
    inner = tanh_coef * (values + cube_coef * values * values * values)
    tangent = jnp.tanh(inner)
    return 0.5 * (1.0 + tangent) + 0.5 * values * (1.0 - tangent * tangent) * tanh_coef * (1.0 + 3.0 * cube_coef * values * values)

def device_sums(left_rows, right_rows):
    left_split = left_rows.reshape(MICRO, N_DP, ROWS, -1).transpose(1, 0, 2, 3).reshape(N_DP, MICRO * ROWS, -1)
    right_split = right_rows.reshape(MICRO, N_DP, ROWS, -1).transpose(1, 0, 2, 3).reshape(N_DP, MICRO * ROWS, -1)
    pieces = jnp.einsum('prs,prd->psd', left_split.astype(jnp.float32), right_split.astype(jnp.float32))
    rounded = lax.optimization_barrier(pieces.astype(jnp.bfloat16)).astype(jnp.float32)
    return lax.optimization_barrier(jnp.sum(rounded, axis=0)) * (1.0 / math.sqrt(MICRO * TOKENS))

def reference(latents, control_hint, upstream, batch_order, section_weight, zero_weight):
    blocks = N_SECTION // 2
    half_width = D // 2
    ordered = jnp.take(latents, batch_order, axis=0).reshape(-1, D)
    hinted = jnp.take(control_hint, batch_order, axis=0).reshape(-1, D)
    current = (ordered.astype(jnp.float32) + hinted.astype(jnp.float32)).astype(jnp.bfloat16)
    states = []
    for block_index in range(blocks):
        product = jnp.dot(current, section_weight[2 * block_index + 1], preferred_element_type=jnp.float32)
        current = (current.astype(jnp.float32) + gelu_value(product)).astype(jnp.bfloat16)
        states.append(current)
    stream = ordered
    slopes = []
    for block_index in range(blocks):
        state_now = states[block_index]
        partial_residual = jnp.dot(state_now[:, half_width:], zero_weight[2 * block_index + 1], preferred_element_type=jnp.float32).astype(jnp.bfloat16)
        partial_back = lax.optimization_barrier(partial_residual).astype(jnp.float32)
        product = jnp.dot(stream, section_weight[2 * block_index], preferred_element_type=jnp.float32)
        residual_add = jnp.dot(state_now[:, :half_width], zero_weight[2 * block_index], preferred_element_type=jnp.float32) + partial_back
        slopes.append(gelu_slope(product))
        stream = (stream.astype(jnp.float32) + gelu_value(product) + residual_add).astype(jnp.bfloat16)
    grad_now = upstream.reshape(-1, D)
    pieces_all = [None] * (2 * blocks)
    for block_index in range(blocks - 1, -1, -1):
        state_now = states[block_index]
        pieces_all[2 * block_index] = device_sums(state_now[:, :half_width], grad_now)
        pieces_all[2 * block_index + 1] = device_sums(state_now[:, half_width:], grad_now)
        if block_index > 0:
            scaled = (grad_now.astype(jnp.float32) * slopes[block_index]).astype(jnp.bfloat16)
            back_term = jnp.dot(scaled, section_weight[2 * block_index].T, preferred_element_type=jnp.float32)
            grad_now = (grad_now.astype(jnp.float32) + back_term).astype(jnp.bfloat16)
    return jnp.stack(pieces_all)
```

```python
import functools
import math

import jax
import jax.numpy as jnp
from jax import lax
from jax.experimental import pallas as pl
from jax.experimental.pallas import tpu as pltpu
from jax.sharding import PartitionSpec as P

tanh_coef = 0.7978845608028654
cube_coef = 0.044715
f32 = jnp.float32
bf16 = jnp.bfloat16


def gelu_parts(values):
    square = values * values
    tangent = jnp.tanh(tanh_coef * (values + cube_coef * square * values))
    return square, tangent


def gelu_value(values):
    _, tangent = gelu_parts(values)
    return 0.5 * values * (1.0 + tangent)


def gelu_slope(values):
    square, tangent = gelu_parts(values)
    return 0.5 * (1.0 + tangent) + 0.5 * values * (1.0 - tangent * tangent) * tanh_coef * (
        1.0 + 3.0 * cube_coef * square
    )


def mm(left, right):
    return jnp.dot(left, right, preferred_element_type=f32)


def kernel(
    blocks, n_dp, order_ref, lat_ref, hint_ref, up_ref, w_hbm, z_hbm, out_ref,
    w, z, flat, chain, mine, side, resid, pout, back, slope, gbuf, et, ecol,
    load_sem, chain_s, chain_r, side_s, side_r, resid_s, resid_r, back_s, back_r,
    e_s, e_r, ag_s, ag_r, sib_s, sib_r,
):
    sections = 2 * blocks
    line = n_dp // 2
    micro, rows, width = lat_ref.shape
    half = width // 2
    padded = flat.shape[0]
    share = et.shape[1]
    place = lax.axis_index("section")
    me = lax.axis_index("dp")
    depth = place // 2
    parity = place % 2
    sibling = place + 1 - 2 * parity
    here, across = me // 2, me % 2
    partner = me + 1 - 2 * across
    is_base = parity == 0
    is_control = parity == 1
    last = depth == blocks - 1

    load_w = pltpu.make_async_copy(w_hbm.at[0], w, load_sem.at[0])
    load_z = pltpu.make_async_copy(z_hbm.at[0], z, load_sem.at[1])
    load_w.start()
    load_z.start()

    barrier = pltpu.get_barrier_semaphore()

    def greet(step, carry):
        pl.semaphore_signal(
            barrier, inc=1, device_id={"dp": lax.rem(me + step, n_dp)},
            device_id_type=pl.DeviceIdType.MESH,
        )
        return carry

    lax.fori_loop(1, n_dp, greet, 0)
    greeted = n_dp - 1
    for step in (-2, -1, 1, 2):
        there = place + step
        inside = (there >= 0) & (there < sections)

        @pl.when(inside)
        def _():
            pl.semaphore_signal(
                barrier, inc=1, device_id={"section": there}, device_id_type=pl.DeviceIdType.MESH
            )

        greeted = greeted + jnp.where(inside, 1, 0)

    def remote(src, dst, send, recv, **where):
        return pltpu.make_async_remote_copy(
            src_ref=src, dst_ref=dst, send_sem=send, recv_sem=recv, device_id=where,
            device_id_type=pl.DeviceIdType.MESH,
        )

    def fill(slot_rows, target):
        flat[padded - 16 :, :] = jnp.zeros((16, width), f32)
        for slot in range(micro):
            flat[slot * rows : (slot + 1) * rows, :] = slot_rows(slot)
        for part in range(2):
            target[part] = flat[:, part * half : (part + 1) * half].astype(bf16)

    @pl.when((depth == 0) & is_base)
    def _():
        fill(lambda slot: lat_ref[order_ref[slot]].astype(f32), chain)

    @pl.when((depth == 0) & is_control)
    def _():
        fill(
            lambda slot: lat_ref[order_ref[slot]].astype(f32) + hint_ref[order_ref[slot]].astype(f32),
            chain,
        )

    @pl.when(last)
    def _():
        fill(lambda slot: up_ref[slot].astype(f32), gbuf.at[me])

    out_ref[...] = jnp.zeros_like(out_ref)
    pl.semaphore_wait(barrier, greeted)

    def go_up(d):
        return remote(gbuf.at[d, parity], gbuf.at[d, parity], ag_s.at[0, d], ag_r.at[d], dp=me + 2)

    def go_down(d):
        return remote(gbuf.at[d, parity], gbuf.at[d, parity], ag_s.at[1, d], ag_r.at[d], dp=me - 2)

    def go_across(d):
        return remote(gbuf.at[d, parity], gbuf.at[d, parity], ag_s.at[2, d], ag_r.at[d], dp=partner)

    def go_sibling(d):
        return remote(gbuf.at[d, parity], gbuf.at[d, parity], sib_s.at[d], sib_r.at[d], section=sibling)

    def arrived(d):
        return remote(gbuf.at[d, parity], gbuf.at[d, parity], ag_s.at[2, d], ag_r.at[d], dp=partner)

    def arrived_sibling(d):
        return remote(
            gbuf.at[d, 1 - parity], gbuf.at[d, 1 - parity], sib_s.at[d], sib_r.at[d], section=sibling
        )

    def gather_start():
        @pl.when(here + 1 < line)
        def _():
            go_up(me).start()

        @pl.when(here > 0)
        def _():
            go_down(me).start()

        go_across(me).start()

    @pl.when(last)
    def _():
        gather_start()

    load_w.wait()
    load_z.wait()

    def product(source, part):
        return sum(
            mm(source[inner], w[inner * half : (inner + 1) * half, part * half : (part + 1) * half])
            for inner in range(2)
        )

    def to_chain(part):
        return remote(mine.at[part], chain.at[part], chain_s.at[part], chain_r.at[part], section=place + 2)

    def from_chain(part):
        return remote(mine.at[part], chain.at[part], chain_s.at[part], chain_r.at[part], section=sibling)

    to_side = remote(mine.at[0], side, side_s, side_r, section=place - 1)
    from_side = remote(mine.at[0], side, side_s, side_r, section=sibling)

    def to_resid(part):
        return remote(pout.at[part], resid.at[part], resid_s.at[part], resid_r.at[part], section=place - 1)

    def from_resid(part):
        return remote(pout.at[part], resid.at[part], resid_s.at[part], resid_r.at[part], section=sibling)

    def to_back(part):
        return remote(back.at[part], gbuf.at[me, part], back_s.at[part], back_r, section=place - 2 + part)

    from_back = remote(back.at[0], gbuf.at[me, parity], back_s.at[0], back_r, section=sibling)

    def spread(columns):
        turned = columns.astype(f32).T
        for d in range(n_dp):
            et[d] = turned[d * share : (d + 1) * share, :].astype(bf16)
        ecol[me] = et[me]

        def send(step, carry):
            there = lax.rem(me + step, n_dp)
            remote(et.at[there], ecol.at[me], e_s.at[step], e_r.at[me], dp=there).start()
            return carry

        lax.fori_loop(1, n_dp, send, 0)

    @pl.when(depth > 0)
    def _():
        from_chain(0).wait_recv()
        from_chain(1).wait_recv()

    @pl.when(is_control)
    def _():
        for part in range(2):
            value = product(chain, part)
            mine[part] = (chain[part].astype(f32) + gelu_value(value)).astype(bf16)
            if part == 0:
                to_side.start()

            @pl.when(jnp.logical_not(last))
            def _():
                to_chain(part).start()

        @pl.when(jnp.logical_not(last))
        def _():
            for part in range(2):
                pout[part] = mm(mine[1], z[:, part * half : (part + 1) * half]).astype(bf16)
                to_resid(part).start()

        spread(mine[1])

        @pl.when(jnp.logical_not(last))
        def _():
            from_back.wait_recv()
            gather_start()
            go_sibling(me).start()

    @pl.when(is_base)
    def _():
        for part in range(2):
            value = product(chain, part)

            @pl.when(depth > 0)
            def _():
                slope[:, part * half : (part + 1) * half] = gelu_slope(value)

            @pl.when(jnp.logical_not(last))
            def _():
                base = chain[part].astype(f32) + gelu_value(value)
                if part == 0:
                    from_side.wait_recv()
                added = mm(side[...], z[:, part * half : (part + 1) * half])
                from_resid(part).wait_recv()
                mine[part] = (base + added + resid[part].astype(f32)).astype(bf16)
                to_chain(part).start()

        @pl.when((depth == 0) & jnp.logical_not(last))
        def _():
            spread(side[...])

        @pl.when(jnp.logical_not(last))
        def _():
            from_back.wait_recv()
            gather_start()
            go_sibling(me).start()

        @pl.when(depth > 0)
        def _():
            @pl.when(jnp.logical_not(last))
            def _():
                arrived_sibling(me).wait_recv()

            scaled = [
                (gbuf[me, part].astype(f32) * slope[:, part * half : (part + 1) * half]).astype(bf16)
                for part in range(2)
            ]
            for part in range(2):
                term = sum(
                    lax.dot_general(
                        scaled[inner],
                        w[part * half : (part + 1) * half, inner * half : (inner + 1) * half],
                        (((1,), (1,)), ((), ())),
                        preferred_element_type=f32,
                    )
                    for inner in range(2)
                )
                back[part] = (gbuf[me, part].astype(f32) + term).astype(bf16)
                to_back(part).start()

        @pl.when((depth > 0) | last)
        def _():
            @pl.when(last)
            def _():
                from_side.wait_recv()

            spread(side[...])

    def add_chunk(d):
        @pl.when(d != me)
        def _():
            remote(et.at[d], ecol.at[d], e_s.at[0], e_r.at[d], dp=partner).wait_recv()

        for part in range(2):
            cut = slice(part * half, (part + 1) * half)
            out_ref[:, cut] += mm(ecol[d], gbuf[d, part])

    def gather_step(reach, carry):
        @pl.when(here - reach >= 0)
        def _():
            d = me - 2 * reach
            arrived(d).wait_recv()

            @pl.when(here + 1 < line)
            def _():
                go_up(d).start()

            go_across(d).start()
            go_sibling(d).start()

        @pl.when(here + reach < line)
        def _():
            d = me + 2 * reach
            arrived(d).wait_recv()

            @pl.when(here > 0)
            def _():
                go_down(d).start()

            go_across(d).start()
            go_sibling(d).start()

        near = reach - 1

        def crossed(shift):
            d = partner + shift
            arrived(d).wait_recv()
            go_sibling(d).start()

        def finish(shift):
            @pl.when(jnp.logical_not((shift == 0) & last) & ((shift != 0) | is_control | (depth == 0)))
            def _():
                arrived_sibling(me + shift).wait_recv()

            add_chunk(me + shift)
            arrived_sibling(partner + shift).wait_recv()
            add_chunk(partner + shift)

        low = here - near >= 0
        high = (here + near < line) & (near > 0)
        for job in (crossed, finish):

            @pl.when(low)
            def _():
                job(-2 * near)

            @pl.when(high)
            def _():
                job(2 * near)

        return carry

    lax.fori_loop(1, line + 1, gather_step, 0)

    @pl.when(is_control)
    def _():
        to_side.wait_send()

        @pl.when(jnp.logical_not(last))
        def _():
            for part in range(2):
                to_resid(part).wait_send()

    @pl.when(jnp.logical_not(last))
    def _():
        for part in range(2):
            to_chain(part).wait_send()

    @pl.when(is_base & (depth > 0))
    def _():
        for part in range(2):
            to_back(part).wait_send()

    def drain(d, carry):
        @pl.when(d > 0)
        def _():
            remote(et.at[d], ecol.at[d], e_s.at[d], e_r.at[d], dp=partner).wait_send()

        @pl.when(d % 2 == across)
        def _():
            @pl.when((d <= me) & (here + 1 < line))
            def _():
                go_up(d).wait_send()

            @pl.when((d >= me) & (here > 0))
            def _():
                go_down(d).wait_send()

            go_across(d).wait_send()

        @pl.when((d != me) | jnp.logical_not(last))
        def _():
            go_sibling(d).wait_send()

        return carry

    lax.fori_loop(0, n_dp, drain, 0)


def body(blocks, n_dp, latents, control_hint, upstream, batch_order, section_weight, zero_weight):
    micro, rows, width = latents.shape
    half = zero_weight.shape[1]
    share = half // n_dp
    padded = (micro * rows + 15) // 16 * 16
    vmem = pl.BlockSpec(memory_space=pltpu.VMEM)
    whole = pl.BlockSpec(memory_space=pl.ANY)
    dma = pltpu.SemaphoreType.DMA
    summed = pl.pallas_call(
        functools.partial(kernel, blocks, n_dp),
        out_shape=jax.ShapeDtypeStruct((share, width), f32),
        in_specs=[pl.BlockSpec(memory_space=pltpu.SMEM), vmem, vmem, vmem, whole, whole],
        out_specs=vmem,
        scratch_shapes=[
            pltpu.VMEM((width, width), bf16),
            pltpu.VMEM((half, width), bf16),
            pltpu.VMEM((padded, width), f32),
            pltpu.VMEM((2, padded, half), bf16),
            pltpu.VMEM((2, padded, half), bf16),
            pltpu.VMEM((padded, half), bf16),
            pltpu.VMEM((2, padded, half), bf16),
            pltpu.VMEM((2, padded, half), bf16),
            pltpu.VMEM((2, padded, half), bf16),
            pltpu.VMEM((padded, width), f32),
            pltpu.VMEM((n_dp, 2, padded, half), bf16),
            pltpu.VMEM((n_dp, share, padded), bf16),
            pltpu.VMEM((n_dp, share, padded), bf16),
            dma((2,)), dma((2,)), dma((2,)), dma, dma, dma((2,)), dma((2,)), dma((2,)), dma,
            dma((n_dp,)), dma((n_dp,)), dma((3, n_dp)), dma((n_dp,)), dma((n_dp,)), dma((n_dp,)),
        ],
        compiler_params=pltpu.CompilerParams(
            collective_id=0, has_side_effects=True, vmem_limit_bytes=50 * 1024 * 1024
        ),
    )(batch_order, latents, control_hint, upstream, section_weight, zero_weight)
    grad_scale = 1.0 / math.sqrt(micro * rows * n_dp)
    return summed[None] * grad_scale


def solution(mesh):
    placed = (
        P(None, "dp", None),
        P(None, "dp", None),
        P(None, "dp", None),
        P(),
        P("section", None, None),
        P("section", None, None),
    )
    return jax.shard_map(
        functools.partial(body, mesh.shape["section"] // 2, mesh.shape["dp"]),
        mesh=mesh, in_specs=placed, out_specs=P("section", "dp", None), check_vma=False,
    )
```

```python
import functools
import math

import jax
import jax.numpy as jnp
from jax import lax
from jax.experimental import pallas as pl
from jax.experimental.pallas import tpu as pltpu
from jax.sharding import PartitionSpec as P

tanh_coef = 0.7978845608028654
cube_coef = 0.044715
f32 = jnp.float32
bf16 = jnp.bfloat16


def gelu_parts(values):
    square = values * values
    tangent = jnp.tanh(tanh_coef * (values + cube_coef * square * values))
    return square, tangent


def gelu_value(values):
    _, tangent = gelu_parts(values)
    return 0.5 * values * (1.0 + tangent)


def gelu_slope(values):
    square, tangent = gelu_parts(values)
    return 0.5 * (1.0 + tangent) + 0.5 * values * (1.0 - tangent * tangent) * tanh_coef * (
        1.0 + 3.0 * cube_coef * square
    )


def mm(left, right):
    return jnp.dot(left, right, preferred_element_type=f32)


def kernel(
    blocks, n_dp, order_any, lat_any, hint_any, up_any, w_any, z_any, out_ref,
    order, lat, hint, up, w, z, flat, chain, mine, side, hside, resid, pout, back, slope, gbuf,
    et, ecol, hacc, hout, ret, load_sem, chain_s, chain_r, side_s, side_r, resid_s, resid_r,
    back_s, back_r, e_s, e_r, ag_s, ag_r, sib_s, sib_r, ret_s, ret_r,
):
    sections = 2 * blocks
    line = n_dp // 2
    early = min(2, line - 1)
    micro, rows, width = lat.shape
    half = width // 2
    quarter = half // 2
    padded = flat.shape[0]
    share = et.shape[2]
    place = lax.axis_index("section")
    me = lax.axis_index("dp")
    depth = place // 2
    parity = place % 2
    sibling = place + 1 - 2 * parity
    here, across = me // 2, me % 2
    partner = me + 1 - 2 * across
    is_base = parity == 0
    is_control = parity == 1
    first = depth == 0
    last = depth == blocks - 1
    cuts = [slice(0, half), slice(half, width)]

    def when(condition):
        return pl.when(condition)

    loads = [
        (first, pltpu.make_async_copy(order_any, order, load_sem.at[0])),
        (first, pltpu.make_async_copy(lat_any, lat, load_sem.at[1])),
        (first & is_control, pltpu.make_async_copy(hint_any, hint, load_sem.at[2])),
        (last, pltpu.make_async_copy(up_any, up, load_sem.at[3])),
    ]
    load_w = pltpu.make_async_copy(w_any.at[0], w, load_sem.at[4])
    load_z = pltpu.make_async_copy(z_any.at[0], z, load_sem.at[5])
    for needed, load in loads:

        @when(needed)
        def _():
            load.start()

    load_w.start()
    load_z.start()

    barrier = pltpu.get_barrier_semaphore()

    def greet(step, carry):
        pl.semaphore_signal(
            barrier, inc=1, device_id={"dp": lax.rem(me + step, n_dp)},
            device_id_type=pl.DeviceIdType.MESH,
        )
        return carry

    lax.fori_loop(1, n_dp, greet, 0)
    greeted = n_dp - 1
    for step in (-2, -1, 1, 2):
        there = place + step
        inside = (there >= 0) & (there < sections)

        @when(inside)
        def _():
            pl.semaphore_signal(
                barrier, inc=1, device_id={"section": there}, device_id_type=pl.DeviceIdType.MESH
            )

        greeted = greeted + jnp.where(inside, 1, 0)

    def remote(src, dst, send, recv, **where):
        return pltpu.make_async_remote_copy(
            src_ref=src, dst_ref=dst, send_sem=send, recv_sem=recv, device_id=where,
            device_id_type=pl.DeviceIdType.MESH,
        )

    for needed, load in loads:

        @when(needed)
        def _():
            load.wait()

    def fill(slot_rows, targets):
        flat[padded - 16 :, :] = jnp.zeros((16, width), f32)
        for slot in range(micro):
            flat[slot * rows : (slot + 1) * rows, :] = slot_rows(slot)
        for part in range(2):
            targets[part][...] = flat[:, cuts[part]].astype(bf16)

    @when(last)
    def _():
        fill(lambda slot: up[slot].astype(f32), [gbuf.at[0, me], gbuf.at[1, me]])

    def fill_first(slot_rows):
        fill(slot_rows, [chain.at[0], chain.at[1]])

    @when(first & is_base)
    def _():
        fill_first(lambda slot: lat[order[slot]].astype(f32))

    @when(first & is_control)
    def _():
        fill_first(lambda slot: lat[order[slot]].astype(f32) + hint[order[slot]].astype(f32))

    pl.semaphore_wait(barrier, greeted)

    def chunk(stream, d, core):
        return gbuf.at[stream, d, :, pl.ds(pl.multiple_of(core * quarter, quarter), quarter)]

    def hop(stream, d, way, **where):
        return remote(
            chunk(stream, d, parity), chunk(stream, d, parity),
            ag_s.at[3 * stream + way, d], ag_r.at[stream, d], **where,
        )

    def go_up(stream, d):
        return hop(stream, d, 0, dp=me + 2)

    def go_down(stream, d):
        return hop(stream, d, 1, dp=me - 2)

    def go_across(stream, d):
        return hop(stream, d, 2, dp=partner)

    def over(stream, d, core):
        return remote(
            chunk(stream, d, core), chunk(stream, d, core),
            sib_s.at[stream, d], sib_r.at[stream, d], section=sibling,
        )

    def go_sibling(stream, d):
        return over(stream, d, parity)

    def gather_start(stream):
        @when(here + 1 < line)
        def _():
            go_up(stream, me).start()

        @when(here > 0)
        def _():
            go_down(stream, me).start()

        go_across(stream, me).start()

    def forward(streams, reach):
        for stream in streams:

            @when(here - reach >= 0)
            def _():
                d = me - 2 * reach
                hop(stream, d, 2, dp=partner).wait_recv()

                @when(here + 1 < line)
                def _():
                    go_up(stream, d).start()

                go_across(stream, d).start()
                go_sibling(stream, d).start()

            @when(here + reach < line)
            def _():
                d = me + 2 * reach
                hop(stream, d, 2, dp=partner).wait_recv()

                @when(here > 0)
                def _():
                    go_down(stream, d).start()

                go_across(stream, d).start()
                go_sibling(stream, d).start()

    def sides(near, job):
        @when(here - near >= 0)
        def _():
            job(-2 * near)

        @when((here + near < line) & (near > 0))
        def _():
            job(2 * near)

    def cross(streams, near):
        def job(shift):
            for stream in streams:
                d = partner + shift
                hop(stream, d, 2, dp=partner).wait_recv()
                go_sibling(stream, d).start()

        sides(near, job)

    def finish(streams, near):
        def job(shift):
            for stream in streams:
                group = stream // 2
                for d in (me + shift, partner + shift):
                    if stream == 0:
                        expected = (d != me) | (jnp.logical_not(last) & (is_control | first))
                    elif stream == 1:
                        expected = d != me
                    else:
                        expected = (d != me) | is_control

                    @when(expected)
                    def _():
                        over(stream, d, 1 - parity).wait_recv()

                    if stream != 1:

                        @when(d != me)
                        def _():
                            remote(
                                et.at[group, d], ecol.at[group, d], e_s.at[group, 0],
                                e_r.at[group, d], dp=partner,
                            ).wait_recv()

                    term = mm(ecol[group, d], gbuf[stream, d])
                    if stream == 2:
                        hacc[...] += term
                    else:
                        out_ref[:, cuts[stream]] += term

        sides(near, job)

    def loop(low, high, step):
        def once(index, carry):
            step(index)
            return carry

        lax.fori_loop(low, high, once, 0)

    def gather_loop(stream):
        def step(reach):
            forward([stream], reach)
            cross([stream], reach - 1)
            finish([stream], reach - 1)

        loop(1, line + 1, step)

    @when(last)
    def _():
        gather_start(0)
        gather_start(1)

    out_ref[...] = jnp.zeros_like(out_ref)
    hacc[...] = jnp.zeros_like(hacc)
    load_w.wait()

    def to_chain(part, target=None):
        target = place + 2 if target is None else target
        return remote(mine.at[part], chain.at[part], chain_s.at[part], chain_r.at[part], section=target)

    def to_side(target):
        return remote(mine.at[0], side, side_s.at[0], side_r.at[0], section=target)

    def to_hside(target):
        return remote(chain.at[0], hside, side_s.at[1], side_r.at[1], section=target)

    def to_resid(part, target):
        return remote(pout.at[part], resid.at[part], resid_s.at[part], resid_r.at[part], section=target)

    def to_back(core, target):
        return remote(
            back.at[:, core * quarter : (core + 1) * quarter], chunk(0, me, core),
            back_s.at[core], back_r.at[0], section=target,
        )

    def to_helper(target):
        return remote(chunk(2, me, 1), chunk(2, me, 1), back_s.at[2], back_r.at[1], section=target)

    def to_earlier(target):
        return remote(gbuf.at[2, me], gbuf.at[1, me], back_s.at[3], back_r.at[2], section=target)

    def to_return(target):
        return remote(hout, ret, ret_s, ret_r, section=target)

    def spread(group, columns):
        turned = columns.astype(f32).T
        for d in range(n_dp):
            et[group, d] = turned[d * share : (d + 1) * share, :].astype(bf16)
        ecol[group, me] = et[group, me]

        def send(step):
            there = lax.rem(me + step, n_dp)
            remote(
                et.at[group, there], ecol.at[group, me], e_s.at[group, step], e_r.at[group, me], dp=there
            ).start()

        loop(1, n_dp, send)

    @when(last)
    def _():
        for reach in range(1, early + 1):
            forward([0, 1], reach)

    @when(is_control)
    def _():
        @when(depth > 0)
        def _():
            to_chain(0, sibling).wait_recv()
            to_hside(sibling).start()
            to_chain(1, sibling).wait_recv()

        for part in range(2):
            value = mm(chain[0], w[:half, cuts[part]]) + mm(chain[1], w[half:, cuts[part]])
            mine[part] = (chain[part].astype(f32) + gelu_value(value)).astype(bf16)
            if part == 0:
                to_side(place - 1).start()

            @when(jnp.logical_not(last))
            def _():
                to_chain(part).start()

        load_z.wait()

        @when(jnp.logical_not(last))
        def _():
            for part in range(2):
                pout[part] = mm(mine[1], z[:, cuts[part]]).astype(bf16)
                to_resid(part, place - 1).start()

        @when(depth > 0)
        def _():
            spread(1, chain[1])

        spread(0, mine[1])

        @when(jnp.logical_not(last))
        def _():
            to_back(1, sibling).wait_recv()
            gather_start(0)
            go_sibling(0, me).start()

        @when(depth > 0)
        def _():
            to_helper(sibling).wait_recv()
            gather_start(2)

    @when(is_base)
    def _():
        @when(depth > 0)
        def _():
            to_hside(sibling).wait_recv()
            spread(1, hside[...])
            to_chain(0, sibling).wait_recv()

        slope[...] = mm(chain[0], w[:half, :])

        @when(depth > 0)
        def _():
            to_chain(1, sibling).wait_recv()

        for part in range(2):
            value = slope[:, cuts[part]] + mm(chain[1], w[half:, cuts[part]])

            @when(depth > 0)
            def _():
                slope[:, cuts[part]] = gelu_slope(value)

            @when(jnp.logical_not(last))
            def _():
                flat[:, cuts[part]] = chain[part].astype(f32) + gelu_value(value)

        load_z.wait()

        @when(jnp.logical_not(last))
        def _():
            to_side(sibling).wait_recv()
            for part in range(2):
                flat[:, cuts[part]] += mm(side[...], z[:, cuts[part]])
            for part in range(2):
                to_resid(part, sibling).wait_recv()
                mine[part] = (flat[:, cuts[part]] + resid[part].astype(f32)).astype(bf16)
                to_chain(part).start()

        @when(first & jnp.logical_not(last))
        def _():
            spread(0, side[...])

        @when(jnp.logical_not(last))
        def _():
            to_back(0, sibling).wait_recv()
            gather_start(0)
            go_sibling(0, me).start()

        @when(depth > 0)
        def _():
            @when(jnp.logical_not(last))
            def _():
                over(0, me, 1).wait_recv()
                to_earlier(sibling).wait_recv()

            scaled = [
                (gbuf[part, me].astype(f32) * slope[:, cuts[part]]).astype(bf16) for part in range(2)
            ]
            for part in range(2):
                term = sum(
                    lax.dot_general(
                        scaled[inner], w[cuts[part], cuts[inner]], (((1,), (1,)), ((), ())),
                        preferred_element_type=f32,
                    )
                    for inner in range(2)
                )
                value = (gbuf[part, me].astype(f32) + term).astype(bf16)
                if part == 0:
                    back[...] = value
                    to_back(0, place - 2).start()
                    to_back(1, place - 1).start()
                else:
                    gbuf[2, me] = value
                    to_helper(sibling).start()
                    gather_start(2)
                    go_sibling(2, me).start()

                    @when(depth > 1)
                    def _():
                        to_earlier(place - 2).start()

        @when((depth > 0) | last)
        def _():
            @when(last)
            def _():
                to_side(sibling).wait_recv()

            spread(0, side[...])

    @when(last)
    def _():
        loop(early + 1, line, lambda reach: forward([0, 1], reach))
        loop(0, early + 1, lambda near: cross([0, 1], near))

    @when(jnp.logical_not(last))
    def _():
        gather_loop(0)

    @when(depth > 0)
    def _():
        gather_loop(2)
        hout[...] = hacc[...].astype(bf16)
        to_return(place - 2).start()

    @when(last)
    def _():
        loop(early + 1, line, lambda near: cross([0, 1], near))
        loop(0, line, lambda near: finish([0, 1], near))

    @when(is_control)
    def _():
        to_side(place - 1).wait_send()

        @when(depth > 0)
        def _():
            to_hside(sibling).wait_send()

        @when(jnp.logical_not(last))
        def _():
            for part in range(2):
                to_resid(part, place - 1).wait_send()

    @when(is_base & (depth > 0))
    def _():
        to_back(0, place - 2).wait_send()
        to_back(1, place - 1).wait_send()
        to_helper(sibling).wait_send()

        @when(depth > 1)
        def _():
            to_earlier(place - 2).wait_send()

    @when(jnp.logical_not(last))
    def _():
        for part in range(2):
            to_chain(part).wait_send()

    def drain(d):
        for stream in range(3):

            @when((True, last, depth > 0)[stream])
            def _():
                @when(d % 2 == across)
                def _():
                    @when((d <= me) & (here + 1 < line))
                    def _():
                        go_up(stream, d).wait_send()

                    @when((d >= me) & (here > 0))
                    def _():
                        go_down(stream, d).wait_send()

                    go_across(stream, d).wait_send()

                @when((d != me) | (jnp.logical_not(last), False, is_base)[stream])
                def _():
                    go_sibling(stream, d).wait_send()

        for group in range(2):

            @when((d > 0) & ((depth > 0) if group else True))
            def _():
                remote(
                    et.at[group, d], ecol.at[group, d], e_s.at[group, d], e_r.at[group, d], dp=partner
                ).wait_send()

    loop(0, n_dp, drain)

    @when(depth > 0)
    def _():
        to_return(place - 2).wait_send()

    @when(jnp.logical_not(last))
    def _():
        to_return(sibling).wait_recv()
        out_ref[:, half:] = ret[...].astype(f32)


def body(blocks, n_dp, latents, control_hint, upstream, batch_order, section_weight, zero_weight):
    micro, rows, width = latents.shape
    half = zero_weight.shape[1]
    share = half // n_dp
    padded = (micro * rows + 15) // 16 * 16
    vmem = pl.BlockSpec(memory_space=pltpu.VMEM)
    whole = pl.BlockSpec(memory_space=pl.ANY)
    dma = pltpu.SemaphoreType.DMA
    summed = pl.pallas_call(
        functools.partial(kernel, blocks, n_dp),
        out_shape=jax.ShapeDtypeStruct((share, width), f32),
        in_specs=[whole] * 6,
        out_specs=vmem,
        scratch_shapes=[
            pltpu.SMEM((micro,), jnp.int32),
            pltpu.VMEM((micro, rows, width), bf16),
            pltpu.VMEM((micro, rows, width), bf16),
            pltpu.VMEM((micro, rows, width), bf16),
            pltpu.VMEM((width, width), bf16),
            pltpu.VMEM((half, width), bf16),
            pltpu.VMEM((padded, width), f32),
            pltpu.VMEM((2, padded, half), bf16),
            pltpu.VMEM((2, padded, half), bf16),
            pltpu.VMEM((padded, half), bf16),
            pltpu.VMEM((padded, half), bf16),
            pltpu.VMEM((2, padded, half), bf16),
            pltpu.VMEM((2, padded, half), bf16),
            pltpu.VMEM((padded, half), bf16),
            pltpu.VMEM((padded, width), f32),
            pltpu.VMEM((3, n_dp, padded, half), bf16),
            pltpu.VMEM((2, n_dp, share, padded), bf16),
            pltpu.VMEM((2, n_dp, share, padded), bf16),
            pltpu.VMEM((share, half), f32),
            pltpu.VMEM((share, half), bf16),
            pltpu.VMEM((share, half), bf16),
            dma((6,)), dma((2,)), dma((2,)), dma((2,)), dma((2,)), dma((2,)), dma((2,)),
            dma((4,)), dma((3,)), dma((2, n_dp)), dma((2, n_dp)), dma((9, n_dp)), dma((3, n_dp)),
            dma((3, n_dp)), dma((3, n_dp)), dma, dma,
        ],
        compiler_params=pltpu.CompilerParams(
            collective_id=0, has_side_effects=True, vmem_limit_bytes=56 * 1024 * 1024
        ),
    )(batch_order, latents, control_hint, upstream, section_weight, zero_weight)
    grad_scale = 1.0 / math.sqrt(micro * rows * n_dp)
    return summed[None] * grad_scale


def solution(mesh):
    placed = (
        P(None, "dp", None),
        P(None, "dp", None),
        P(None, "dp", None),
        P(),
        P("section", None, None),
        P("section", None, None),
    )
    return jax.shard_map(
        functools.partial(body, mesh.shape["section"] // 2, mesh.shape["dp"]),
        mesh=mesh, in_specs=placed, out_specs=P("section", "dp", None), check_vma=False,
    )
```

```python
import functools
import math

import jax
import jax.numpy as jnp
from jax import lax
from jax.experimental import pallas as pl
from jax.experimental.pallas import tpu as pltpu
from jax.sharding import PartitionSpec as P

tanh_coef = 0.7978845608028654
cube_coef = 0.044715
f32 = jnp.float32
bf16 = jnp.bfloat16


def gelu_parts(values):
    square = values * values
    tangent = jnp.tanh(tanh_coef * (values + cube_coef * square * values))
    return square, tangent


def gelu_value(values):
    _, tangent = gelu_parts(values)
    return 0.5 * values * (1.0 + tangent)


def gelu_slope(values):
    square, tangent = gelu_parts(values)
    return 0.5 * (1.0 + tangent) + 0.5 * values * (1.0 - tangent * tangent) * tanh_coef * (
        1.0 + 3.0 * cube_coef * square
    )


def mm(left, right):
    return jnp.dot(left, right, preferred_element_type=f32)


def kernel(
    blocks, n_dp, order_any, lat_any, hint_any, up_any, w_any, z_any, out_ref,
    order, lat, hint, up, w, z, flat, chain, mine, side, hside, resid, pout, back, slope, gbuf,
    et, ecol, hacc, hout, ret, load_sem, chain_s, chain_r, side_s, side_r, resid_s, resid_r,
    back_s, back_r, e_s, e_r, ag_s, ag_r, sib_s, sib_r, ret_s, ret_r,
):
    sections = 2 * blocks
    line = n_dp // 2
    early = min(1, line - 1)
    micro, rows, width = lat.shape
    half = width // 2
    padded = flat.shape[0]
    share = et.shape[2]
    place = lax.axis_index("section")
    me = lax.axis_index("dp")
    depth = place // 2
    parity = place % 2
    sibling = place + 1 - 2 * parity
    here, across = me // 2, me % 2
    partner = me + 1 - 2 * across
    is_base = parity == 0
    is_control = parity == 1
    first = depth == 0
    last = depth == blocks - 1
    cuts = [slice(0, half), slice(half, width)]

    def when(condition):
        return pl.when(condition)

    loads = [
        (first, pltpu.make_async_copy(order_any, order, load_sem.at[0])),
        (first, pltpu.make_async_copy(lat_any, lat, load_sem.at[1])),
        (first & is_control, pltpu.make_async_copy(hint_any, hint, load_sem.at[2])),
        (last, pltpu.make_async_copy(up_any, up, load_sem.at[3])),
    ]
    load_w = pltpu.make_async_copy(w_any.at[0], w, load_sem.at[4])
    load_z = pltpu.make_async_copy(z_any.at[0], z, load_sem.at[5])
    for needed, load in loads:

        @when(needed)
        def _():
            load.start()

    load_w.start()
    load_z.start()

    barrier = pltpu.get_barrier_semaphore()

    def greet(step, carry):
        pl.semaphore_signal(
            barrier, inc=1, device_id={"dp": lax.rem(me + step, n_dp)},
            device_id_type=pl.DeviceIdType.MESH,
        )
        return carry

    lax.fori_loop(1, n_dp, greet, 0)
    greeted = n_dp - 1
    for step in (-2, -1, 1, 2):
        there = place + step
        inside = (there >= 0) & (there < sections)

        @when(inside)
        def _():
            pl.semaphore_signal(
                barrier, inc=1, device_id={"section": there}, device_id_type=pl.DeviceIdType.MESH
            )

        greeted = greeted + jnp.where(inside, 1, 0)

    def remote(src, dst, send, recv, **where):
        return pltpu.make_async_remote_copy(
            src_ref=src, dst_ref=dst, send_sem=send, recv_sem=recv, device_id=where,
            device_id_type=pl.DeviceIdType.MESH,
        )

    for needed, load in loads:

        @when(needed)
        def _():
            load.wait()

    def fill(slot_rows, targets):
        flat[padded - 16 :, :] = jnp.zeros((16, width), f32)
        for slot in range(micro):
            flat[slot * rows : (slot + 1) * rows, :] = slot_rows(slot)
        for part in range(2):
            targets[part][...] = flat[:, cuts[part]].astype(bf16)

    @when(last)
    def _():
        fill(lambda slot: up[slot].astype(f32), [gbuf.at[0, me], gbuf.at[1, me]])

    def fill_first(slot_rows):
        fill(slot_rows, [chain.at[0], chain.at[1]])

    @when(first & is_base)
    def _():
        fill_first(lambda slot: lat[order[slot]].astype(f32))

    @when(first & is_control)
    def _():
        fill_first(lambda slot: lat[order[slot]].astype(f32) + hint[order[slot]].astype(f32))

    pl.semaphore_wait(barrier, greeted)

    def hop(stream, d, way, **where):
        return remote(
            gbuf.at[stream, d], gbuf.at[stream, d],
            ag_s.at[3 * stream + way, d], ag_r.at[stream, d], **where,
        )

    def go_up(stream, d):
        return hop(stream, d, 0, dp=me + 2)

    def go_down(stream, d):
        return hop(stream, d, 1, dp=me - 2)

    def go_across(stream, d):
        return hop(stream, d, 2, dp=partner)

    def go_sibling(stream, d):
        return remote(
            gbuf.at[stream, d], gbuf.at[stream, d], sib_s.at[stream, d], sib_r.at[stream, d], section=sibling
        )

    def gather_start(stream):
        @when(here + 1 < line)
        def _():
            go_up(stream, me).start()

        @when(here > 0)
        def _():
            go_down(stream, me).start()

        go_across(stream, me).start()

    def forward(streams, reach):
        for stream in streams:

            @when(here - reach >= 0)
            def _():
                d = me - 2 * reach
                hop(stream, d, 2, dp=partner).wait_recv()

                @when(here + 1 < line)
                def _():
                    go_up(stream, d).start()

                go_across(stream, d).start()
                go_sibling(stream, d).start()

            @when(here + reach < line)
            def _():
                d = me + 2 * reach
                hop(stream, d, 2, dp=partner).wait_recv()

                @when(here > 0)
                def _():
                    go_down(stream, d).start()

                go_across(stream, d).start()
                go_sibling(stream, d).start()

    def sides(near, job):
        @when(here - near >= 0)
        def _():
            job(-2 * near)

        @when((here + near < line) & (near > 0))
        def _():
            job(2 * near)

    def cross(streams, near):
        def job(shift):
            for stream in streams:
                d = partner + shift
                hop(stream, d, 2, dp=partner).wait_recv()
                go_sibling(stream, d).start()

        sides(near, job)

    def finish(streams, near):
        def job(shift):
            for stream in streams:
                group = stream // 2
                for d in (me + shift, partner + shift):
                    if stream == 2:
                        given = is_control
                    elif stream == 1:
                        given = is_base & (d != me)
                    else:
                        given = is_base & ((d != me) | (first & jnp.logical_not(last)))

                    @when(given)
                    def _():
                        go_sibling(stream, d).wait_recv()

                    if stream != 1:

                        @when(d != me)
                        def _():
                            remote(
                                et.at[group, d], ecol.at[group, d], e_s.at[group, 0],
                                e_r.at[group, d], dp=partner,
                            ).wait_recv()

                    term = mm(ecol[group, d], gbuf[stream, d])
                    if stream == 2:
                        hacc[...] += term
                    else:
                        out_ref[:, cuts[stream]] += term

        sides(near, job)

    def loop(low, high, step):
        def once(index, carry):
            step(index)
            return carry

        lax.fori_loop(low, high, once, 0)

    def gather_loop(stream):
        def step(reach):
            forward([stream], reach)
            cross([stream], reach - 1)
            finish([stream], reach - 1)

        loop(1, line + 1, step)

    def finish_loop(streams):
        loop(0, line, lambda near: finish(streams, near))

    @when(last & is_control)
    def _():
        gather_start(0)
        gather_start(1)

    out_ref[...] = jnp.zeros_like(out_ref)
    hacc[...] = jnp.zeros_like(hacc)
    load_w.wait()

    def to_chain(part, target=None):
        target = place + 2 if target is None else target
        return remote(mine.at[part], chain.at[part], chain_s.at[part], chain_r.at[part], section=target)

    def to_side(target):
        return remote(mine.at[0], side, side_s.at[0], side_r.at[0], section=target)

    def to_hside(target):
        return remote(chain.at[0], hside, side_s.at[1], side_r.at[1], section=target)

    def to_resid(part, target):
        return remote(pout.at[part], resid.at[part], resid_s.at[part], resid_r.at[part], section=target)

    def to_back(target):
        return remote(back, gbuf.at[0, me], back_s.at[0], back_r.at[0], section=target)

    def to_earlier(target):
        return remote(gbuf.at[2, me], gbuf.at[1, me], back_s.at[1], back_r.at[1], section=target)

    def to_return(target):
        return remote(hout, ret, ret_s, ret_r, section=target)

    def spread(group, columns):
        turned = columns.astype(f32).T
        for d in range(n_dp):
            et[group, d] = turned[d * share : (d + 1) * share, :].astype(bf16)
        ecol[group, me] = et[group, me]

        def send(step):
            there = lax.rem(me + step, n_dp)
            remote(
                et.at[group, there], ecol.at[group, me], e_s.at[group, step], e_r.at[group, me], dp=there
            ).start()

        loop(1, n_dp, send)

    @when(last & is_control)
    def _():
        for reach in range(1, early + 1):
            forward([0, 1], reach)

    @when(is_control)
    def _():
        @when(depth > 0)
        def _():
            to_chain(0, sibling).wait_recv()
            to_hside(sibling).start()
            to_chain(1, sibling).wait_recv()

        for part in range(2):
            value = mm(chain[0], w[:half, cuts[part]]) + mm(chain[1], w[half:, cuts[part]])
            mine[part] = (chain[part].astype(f32) + gelu_value(value)).astype(bf16)
            if part == 0:
                to_side(place - 1).start()

            @when(jnp.logical_not(last))
            def _():
                to_chain(part).start()

        load_z.wait()

        @when(jnp.logical_not(last))
        def _():
            for part in range(2):
                pout[part] = mm(mine[1], z[:, cuts[part]]).astype(bf16)
                to_resid(part, place - 1).start()

        @when(depth > 0)
        def _():
            spread(1, chain[1])

        spread(0, mine[1])

        @when(jnp.logical_not(last))
        def _():
            to_back(sibling).wait_recv()
            gather_start(0)
            go_sibling(0, me).start()
            gather_loop(0)

        @when(last)
        def _():
            loop(early + 1, line, lambda reach: forward([0, 1], reach))
            loop(0, line, lambda near: cross([0, 1], near))
            finish_loop([0, 1])

        @when(depth > 0)
        def _():
            finish_loop([2])

    @when(is_base)
    def _():
        @when(depth > 0)
        def _():
            to_hside(sibling).wait_recv()
            spread(1, hside[...])
            to_chain(0, sibling).wait_recv()

        slope[...] = mm(chain[0], w[:half, :])

        @when(depth > 0)
        def _():
            to_chain(1, sibling).wait_recv()

        for part in range(2):
            value = slope[:, cuts[part]] + mm(chain[1], w[half:, cuts[part]])

            @when(depth > 0)
            def _():
                slope[:, cuts[part]] = gelu_slope(value)

            @when(jnp.logical_not(last))
            def _():
                flat[:, cuts[part]] = chain[part].astype(f32) + gelu_value(value)

        load_z.wait()

        @when(jnp.logical_not(last))
        def _():
            to_side(sibling).wait_recv()
            for part in range(2):
                flat[:, cuts[part]] += mm(side[...], z[:, cuts[part]])
            for part in range(2):
                to_resid(part, sibling).wait_recv()
                mine[part] = (flat[:, cuts[part]] + resid[part].astype(f32)).astype(bf16)
                to_chain(part).start()

        @when(first & jnp.logical_not(last))
        def _():
            spread(0, side[...])

        @when(depth > 0)
        def _():
            @when(jnp.logical_not(last))
            def _():
                go_sibling(0, me).wait_recv()
                to_earlier(sibling).wait_recv()

            scaled = [
                (gbuf[part, me].astype(f32) * slope[:, cuts[part]]).astype(bf16) for part in range(2)
            ]
            for part in range(2):
                term = sum(
                    lax.dot_general(
                        scaled[inner], w[cuts[part], cuts[inner]], (((1,), (1,)), ((), ())),
                        preferred_element_type=f32,
                    )
                    for inner in range(2)
                )
                value = (gbuf[part, me].astype(f32) + term).astype(bf16)
                if part == 0:
                    back[...] = value
                    to_back(place - 1).start()
                else:
                    gbuf[2, me] = value
                    gather_start(2)
                    go_sibling(2, me).start()

                    @when(depth > 1)
                    def _():
                        to_earlier(place - 2).start()

        @when((depth > 0) | last)
        def _():
            @when(last)
            def _():
                to_side(sibling).wait_recv()

            spread(0, side[...])

        @when(depth > 0)
        def _():
            gather_loop(2)

    @when(depth > 0)
    def _():
        hout[...] = hacc[...].astype(bf16)
        to_return(place - 2).start()

    @when(is_base)
    def _():
        finish_loop([0])

    @when(is_base & last)
    def _():
        finish_loop([1])

    @when(is_control)
    def _():
        to_side(place - 1).wait_send()

        @when(depth > 0)
        def _():
            to_hside(sibling).wait_send()

        @when(jnp.logical_not(last))
        def _():
            for part in range(2):
                to_resid(part, place - 1).wait_send()

    @when(is_base & (depth > 0))
    def _():
        to_back(place - 1).wait_send()

        @when(depth > 1)
        def _():
            to_earlier(place - 2).wait_send()

    @when(jnp.logical_not(last))
    def _():
        for part in range(2):
            to_chain(part).wait_send()

    def drain(d):
        for stream in range(3):

            @when((is_control, is_control & last, is_base & (depth > 0))[stream])
            def _():
                @when(d % 2 == across)
                def _():
                    @when((d <= me) & (here + 1 < line))
                    def _():
                        go_up(stream, d).wait_send()

                    @when((d >= me) & (here > 0))
                    def _():
                        go_down(stream, d).wait_send()

                    go_across(stream, d).wait_send()

                @when((d != me) | (jnp.logical_not(last), False, True)[stream])
                def _():
                    go_sibling(stream, d).wait_send()

        for group in range(2):

            @when((d > 0) & ((depth > 0) if group else True))
            def _():
                remote(
                    et.at[group, d], ecol.at[group, d], e_s.at[group, d], e_r.at[group, d], dp=partner
                ).wait_send()

    loop(0, n_dp, drain)

    @when(depth > 0)
    def _():
        to_return(place - 2).wait_send()

    @when(jnp.logical_not(last))
    def _():
        to_return(sibling).wait_recv()
        out_ref[:, half:] = ret[...].astype(f32)


def body(blocks, n_dp, latents, control_hint, upstream, batch_order, section_weight, zero_weight):
    micro, rows, width = latents.shape
    half = zero_weight.shape[1]
    share = half // n_dp
    padded = (micro * rows + 15) // 16 * 16
    vmem = pl.BlockSpec(memory_space=pltpu.VMEM)
    whole = pl.BlockSpec(memory_space=pl.ANY)
    dma = pltpu.SemaphoreType.DMA
    summed = pl.pallas_call(
        functools.partial(kernel, blocks, n_dp),
        out_shape=jax.ShapeDtypeStruct((share, width), f32),
        in_specs=[whole] * 6,
        out_specs=vmem,
        scratch_shapes=[
            pltpu.SMEM((micro,), jnp.int32),
            pltpu.VMEM((micro, rows, width), bf16),
            pltpu.VMEM((micro, rows, width), bf16),
            pltpu.VMEM((micro, rows, width), bf16),
            pltpu.VMEM((width, width), bf16),
            pltpu.VMEM((half, width), bf16),
            pltpu.VMEM((padded, width), f32),
            pltpu.VMEM((2, padded, half), bf16),
            pltpu.VMEM((2, padded, half), bf16),
            pltpu.VMEM((padded, half), bf16),
            pltpu.VMEM((padded, half), bf16),
            pltpu.VMEM((2, padded, half), bf16),
            pltpu.VMEM((2, padded, half), bf16),
            pltpu.VMEM((padded, half), bf16),
            pltpu.VMEM((padded, width), f32),
            pltpu.VMEM((3, n_dp, padded, half), bf16),
            pltpu.VMEM((2, n_dp, share, padded), bf16),
            pltpu.VMEM((2, n_dp, share, padded), bf16),
            pltpu.VMEM((share, half), f32),
            pltpu.VMEM((share, half), bf16),
            pltpu.VMEM((share, half), bf16),
            dma((6,)), dma((2,)), dma((2,)), dma((2,)), dma((2,)), dma((2,)), dma((2,)),
            dma((2,)), dma((2,)), dma((2, n_dp)), dma((2, n_dp)), dma((9, n_dp)), dma((3, n_dp)),
            dma((3, n_dp)), dma((3, n_dp)), dma, dma,
        ],
        compiler_params=pltpu.CompilerParams(
            collective_id=0, has_side_effects=True, vmem_limit_bytes=56 * 1024 * 1024
        ),
    )(batch_order, latents, control_hint, upstream, section_weight, zero_weight)
    grad_scale = 1.0 / math.sqrt(micro * rows * n_dp)
    return summed[None] * grad_scale


def solution(mesh):
    placed = (
        P(None, "dp", None),
        P(None, "dp", None),
        P(None, "dp", None),
        P(),
        P("section", None, None),
        P("section", None, None),
    )
    return jax.shard_map(
        functools.partial(body, mesh.shape["section"] // 2, mesh.shape["dp"]),
        mesh=mesh, in_specs=placed, out_specs=P("section", "dp", None), check_vma=False,
    )
```

```python
import functools
import math

import jax
import jax.numpy as jnp
from jax import lax
from jax.experimental import pallas as pl
from jax.experimental.pallas import tpu as pltpu
from jax.sharding import PartitionSpec as P

tanh_coef = 0.7978845608028654
cube_coef = 0.044715
f32 = jnp.float32
bf16 = jnp.bfloat16


def gelu_parts(values):
    square = values * values
    tangent = jnp.tanh(tanh_coef * (values + cube_coef * square * values))
    return square, tangent


def gelu_value(values):
    _, tangent = gelu_parts(values)
    return 0.5 * values * (1.0 + tangent)


def gelu_slope(values):
    square, tangent = gelu_parts(values)
    return 0.5 * (1.0 + tangent) + 0.5 * values * (1.0 - tangent * tangent) * tanh_coef * (
        1.0 + 3.0 * cube_coef * square
    )


def mm(left, right):
    return jnp.dot(left, right, preferred_element_type=f32)


def kernel(
    blocks, n_dp, order_any, lat_any, hint_any, up_any, w_any, z_any, out_ref,
    order, lat, hint, up, w, z, flat, chain, mine, side, hside, resid, pout, back, slope, gbuf,
    et, ecol, hacc, hout, ret, load_sem, chain_s, chain_r, side_s, side_r, resid_s, resid_r,
    back_s, back_r, e_s, e_r, ag_s, ag_r, sib_s, sib_r, ret_s, ret_r,
):
    sections = 2 * blocks
    line = n_dp // 2
    early = min(1, line - 1)
    micro, rows, width = lat.shape
    half = width // 2
    padded = flat.shape[0]
    share = hout.shape[0]
    lanes = et.shape[3]
    extra = padded - lanes
    place = lax.axis_index("section")
    me = lax.axis_index("dp")
    depth = place // 2
    parity = place % 2
    sibling = place + 1 - 2 * parity
    here, across = me // 2, me % 2
    partner = me + 1 - 2 * across
    is_base = parity == 0
    is_control = parity == 1
    first = depth == 0
    last = depth == blocks - 1
    cuts = [slice(0, half), slice(half, width)]

    def when(condition):
        return pl.when(condition)

    loads = [
        (first, pltpu.make_async_copy(order_any, order, load_sem.at[0])),
        (first, pltpu.make_async_copy(lat_any, lat, load_sem.at[1])),
        (first & is_control, pltpu.make_async_copy(hint_any, hint, load_sem.at[2])),
        (last, pltpu.make_async_copy(up_any, up, load_sem.at[3])),
    ]
    load_w = pltpu.make_async_copy(w_any.at[0], w, load_sem.at[4])
    load_z = pltpu.make_async_copy(z_any.at[0], z, load_sem.at[5])
    for needed, load in loads:

        @when(needed)
        def _():
            load.start()

    load_w.start()
    load_z.start()

    barrier = pltpu.get_barrier_semaphore()

    def greet(step, carry):
        pl.semaphore_signal(
            barrier, inc=1, device_id={"dp": lax.rem(me + step, n_dp)},
            device_id_type=pl.DeviceIdType.MESH,
        )
        return carry

    lax.fori_loop(1, n_dp, greet, 0)
    greeted = n_dp - 1
    for step in (-2, -1, 1, 2):
        there = place + step
        inside = (there >= 0) & (there < sections)

        @when(inside)
        def _():
            pl.semaphore_signal(
                barrier, inc=1, device_id={"section": there}, device_id_type=pl.DeviceIdType.MESH
            )

        greeted = greeted + jnp.where(inside, 1, 0)

    def remote(src, dst, send, recv, **where):
        return pltpu.make_async_remote_copy(
            src_ref=src, dst_ref=dst, send_sem=send, recv_sem=recv, device_id=where,
            device_id_type=pl.DeviceIdType.MESH,
        )

    for needed, load in loads:

        @when(needed)
        def _():
            load.wait()

    def fill(slot_rows, targets):
        flat[padded - 16 :, :] = jnp.zeros((16, width), f32)
        for slot in range(micro):
            flat[slot * rows : (slot + 1) * rows, :] = slot_rows(slot)
        for part in range(2):
            targets[part][...] = flat[:, cuts[part]].astype(bf16)

    @when(last)
    def _():
        fill(lambda slot: up[slot].astype(f32), [gbuf.at[0, me], gbuf.at[1, me]])

    def fill_first(slot_rows):
        fill(slot_rows, [chain.at[0], chain.at[1]])

    @when(first & is_base)
    def _():
        fill_first(lambda slot: lat[order[slot]].astype(f32))

    @when(first & is_control)
    def _():
        fill_first(lambda slot: lat[order[slot]].astype(f32) + hint[order[slot]].astype(f32))

    pl.semaphore_wait(barrier, greeted)

    def hop(stream, d, way, **where):
        return remote(
            gbuf.at[stream, d], gbuf.at[stream, d],
            ag_s.at[3 * stream + way, d], ag_r.at[stream, d], **where,
        )

    def go_up(stream, d):
        return hop(stream, d, 0, dp=me + 2)

    def go_down(stream, d):
        return hop(stream, d, 1, dp=me - 2)

    def go_across(stream, d):
        return hop(stream, d, 2, dp=partner)

    def go_sibling(stream, d):
        return remote(
            gbuf.at[stream, d], gbuf.at[stream, d], sib_s.at[stream, d], sib_r.at[stream, d], section=sibling
        )

    def gather_start(stream):
        @when(here + 1 < line)
        def _():
            go_up(stream, me).start()

        @when(here > 0)
        def _():
            go_down(stream, me).start()

        go_across(stream, me).start()

    def forward(streams, reach):
        for stream in streams:

            @when(here - reach >= 0)
            def _():
                d = me - 2 * reach
                hop(stream, d, 2, dp=partner).wait_recv()

                @when(here + 1 < line)
                def _():
                    go_up(stream, d).start()

                go_across(stream, d).start()
                go_sibling(stream, d).start()

            @when(here + reach < line)
            def _():
                d = me + 2 * reach
                hop(stream, d, 2, dp=partner).wait_recv()

                @when(here > 0)
                def _():
                    go_down(stream, d).start()

                go_across(stream, d).start()
                go_sibling(stream, d).start()

    def sides(near, job):
        @when(here - near >= 0)
        def _():
            job(-2 * near)

        @when((here + near < line) & (near > 0))
        def _():
            job(2 * near)

    def cross(streams, near):
        def job(shift):
            for stream in streams:
                d = partner + shift
                hop(stream, d, 2, dp=partner).wait_recv()
                go_sibling(stream, d).start()

        sides(near, job)

    def finish(streams, near):
        def job(shift):
            for stream in streams:
                group = stream // 2
                for d in (me + shift, partner + shift):
                    if stream == 2:
                        given = is_control
                    elif stream == 1:
                        given = is_base & (d != me)
                    else:
                        given = is_base & ((d != me) | (first & jnp.logical_not(last)))

                    @when(given)
                    def _():
                        go_sibling(stream, d).wait_recv()

                    if stream != 1:

                        @when(d != me)
                        def _():
                            remote(
                                et.at[group, d], ecol.at[group, d], e_s.at[group, 0],
                                e_r.at[group, d], dp=partner,
                            ).wait_recv()

                    term = mm(ecol[group, d, extra:, :], gbuf[stream, d, :lanes, :])
                    rest = ecol[group, d, :extra, :].astype(f32).T[:share, :].astype(bf16)
                    term = term + mm(rest, gbuf[stream, d, lanes:, :])
                    if stream == 2:
                        hacc[...] += term
                    else:
                        out_ref[:, cuts[stream]] += term

        sides(near, job)

    def loop(low, high, step):
        def once(index, carry):
            step(index)
            return carry

        lax.fori_loop(low, high, once, 0)

    def gather_loop(stream):
        def step(reach):
            forward([stream], reach)
            cross([stream], reach - 1)
            finish([stream], reach - 1)

        loop(1, line + 1, step)

    def finish_loop(streams):
        loop(0, line, lambda near: finish(streams, near))

    @when(last & is_control)
    def _():
        gather_start(0)
        gather_start(1)

    out_ref[...] = jnp.zeros_like(out_ref)
    et[...] = jnp.zeros_like(et)
    hacc[...] = jnp.zeros_like(hacc)
    load_w.wait()

    def to_chain(part, target=None):
        target = place + 2 if target is None else target
        return remote(mine.at[part], chain.at[part], chain_s.at[part], chain_r.at[part], section=target)

    def to_side(target):
        return remote(mine.at[0], side, side_s.at[0], side_r.at[0], section=target)

    def to_hside(target):
        return remote(chain.at[0], hside, side_s.at[1], side_r.at[1], section=target)

    def to_resid(part, target):
        return remote(pout.at[part], resid.at[part], resid_s.at[part], resid_r.at[part], section=target)

    def to_back(target):
        return remote(back, gbuf.at[0, me], back_s.at[0], back_r.at[0], section=target)

    def to_earlier(target):
        return remote(gbuf.at[2, me], gbuf.at[1, me], back_s.at[1], back_r.at[1], section=target)

    def to_return(target):
        return remote(hout, ret, ret_s, ret_r, section=target)

    def spread(group, columns):
        wide = columns.astype(f32)
        turned = wide[:lanes, :].T
        for d in range(n_dp):
            mine_rows = slice(d * share, (d + 1) * share)
            et[group, d, :extra, :share] = wide[lanes:, mine_rows].astype(bf16)
            et[group, d, extra:, :] = turned[mine_rows, :].astype(bf16)
        ecol[group, me] = et[group, me]

        def send(step):
            there = lax.rem(me + step, n_dp)
            remote(
                et.at[group, there], ecol.at[group, me], e_s.at[group, step], e_r.at[group, me], dp=there
            ).start()

        loop(1, n_dp, send)

    @when(last & is_control)
    def _():
        for reach in range(1, early + 1):
            forward([0, 1], reach)

    @when(is_control)
    def _():
        @when(depth > 0)
        def _():
            to_chain(0, sibling).wait_recv()
            to_hside(sibling).start()
            to_chain(1, sibling).wait_recv()

        for part in range(2):
            value = mm(chain[0], w[:half, cuts[part]]) + mm(chain[1], w[half:, cuts[part]])
            mine[part] = (chain[part].astype(f32) + gelu_value(value)).astype(bf16)
            if part == 0:
                to_side(place - 1).start()

            @when(jnp.logical_not(last))
            def _():
                to_chain(part).start()

        load_z.wait()

        @when(jnp.logical_not(last))
        def _():
            for part in range(2):
                pout[part] = mm(mine[1], z[:, cuts[part]]).astype(bf16)
                to_resid(part, place - 1).start()

        @when(depth > 0)
        def _():
            spread(1, chain[1])

        spread(0, mine[1])

        @when(jnp.logical_not(last))
        def _():
            to_back(sibling).wait_recv()
            gather_start(0)
            go_sibling(0, me).start()
            gather_loop(0)

        @when(last)
        def _():
            loop(early + 1, line, lambda reach: forward([0, 1], reach))
            loop(0, line, lambda near: cross([0, 1], near))
            finish_loop([0, 1])

        @when(depth > 0)
        def _():
            finish_loop([2])

    @when(is_base)
    def _():
        @when(depth > 0)
        def _():
            to_hside(sibling).wait_recv()
            spread(1, hside[...])
            to_chain(0, sibling).wait_recv()

        slope[...] = mm(chain[0], w[:half, :])

        @when(depth > 0)
        def _():
            to_chain(1, sibling).wait_recv()

        for part in range(2):
            value = slope[:, cuts[part]] + mm(chain[1], w[half:, cuts[part]])

            @when(depth > 0)
            def _():
                slope[:, cuts[part]] = gelu_slope(value)

            @when(jnp.logical_not(last))
            def _():
                flat[:, cuts[part]] = chain[part].astype(f32) + gelu_value(value)

        load_z.wait()

        @when(jnp.logical_not(last))
        def _():
            to_side(sibling).wait_recv()
            for part in range(2):
                flat[:, cuts[part]] += mm(side[...], z[:, cuts[part]])
            for part in range(2):
                to_resid(part, sibling).wait_recv()
                mine[part] = (flat[:, cuts[part]] + resid[part].astype(f32)).astype(bf16)
                to_chain(part).start()

        @when(first & jnp.logical_not(last))
        def _():
            spread(0, side[...])

        @when(depth > 0)
        def _():
            @when(jnp.logical_not(last))
            def _():
                go_sibling(0, me).wait_recv()
                to_earlier(sibling).wait_recv()

            scaled = [
                (gbuf[part, me].astype(f32) * slope[:, cuts[part]]).astype(bf16) for part in range(2)
            ]
            for part in range(2):
                term = sum(
                    lax.dot_general(
                        scaled[inner], w[cuts[part], cuts[inner]], (((1,), (1,)), ((), ())),
                        preferred_element_type=f32,
                    )
                    for inner in range(2)
                )
                value = (gbuf[part, me].astype(f32) + term).astype(bf16)
                if part == 0:
                    back[...] = value
                    to_back(place - 1).start()
                else:
                    gbuf[2, me] = value
                    gather_start(2)
                    go_sibling(2, me).start()

                    @when(depth > 1)
                    def _():
                        to_earlier(place - 2).start()

        @when(depth > 0)
        def _():
            @when(jnp.logical_not(last))
            def _():
                spread(0, side[...])

            gather_loop(2)

    @when(depth > 0)
    def _():
        hout[...] = hacc[...].astype(bf16)
        to_return(place - 2).start()

    @when(is_base & last)
    def _():
        to_side(sibling).wait_recv()
        spread(0, side[...])

    @when(is_base)
    def _():
        finish_loop([0])

    @when(is_base & last)
    def _():
        finish_loop([1])

    @when(is_control)
    def _():
        to_side(place - 1).wait_send()

        @when(depth > 0)
        def _():
            to_hside(sibling).wait_send()

        @when(jnp.logical_not(last))
        def _():
            for part in range(2):
                to_resid(part, place - 1).wait_send()

    @when(is_base & (depth > 0))
    def _():
        to_back(place - 1).wait_send()

        @when(depth > 1)
        def _():
            to_earlier(place - 2).wait_send()

    @when(jnp.logical_not(last))
    def _():
        for part in range(2):
            to_chain(part).wait_send()

    def drain(d):
        for stream in range(3):

            @when((is_control, is_control & last, is_base & (depth > 0))[stream])
            def _():
                @when(d % 2 == across)
                def _():
                    @when((d <= me) & (here + 1 < line))
                    def _():
                        go_up(stream, d).wait_send()

                    @when((d >= me) & (here > 0))
                    def _():
                        go_down(stream, d).wait_send()

                    go_across(stream, d).wait_send()

                @when((d != me) | (jnp.logical_not(last), False, True)[stream])
                def _():
                    go_sibling(stream, d).wait_send()

        for group in range(2):

            @when((d > 0) & ((depth > 0) if group else True))
            def _():
                remote(
                    et.at[group, d], ecol.at[group, d], e_s.at[group, d], e_r.at[group, d], dp=partner
                ).wait_send()

    loop(0, n_dp, drain)

    @when(depth > 0)
    def _():
        to_return(place - 2).wait_send()

    @when(jnp.logical_not(last))
    def _():
        to_return(sibling).wait_recv()
        out_ref[:, half:] = ret[...].astype(f32)


def body(blocks, n_dp, latents, control_hint, upstream, batch_order, section_weight, zero_weight):
    micro, rows, width = latents.shape
    half = zero_weight.shape[1]
    share = half // n_dp
    padded = (micro * rows + 15) // 16 * 16
    lanes = padded // 128 * 128
    vmem = pl.BlockSpec(memory_space=pltpu.VMEM)
    whole = pl.BlockSpec(memory_space=pl.ANY)
    dma = pltpu.SemaphoreType.DMA
    summed = pl.pallas_call(
        functools.partial(kernel, blocks, n_dp),
        out_shape=jax.ShapeDtypeStruct((share, width), f32),
        in_specs=[whole] * 6,
        out_specs=vmem,
        scratch_shapes=[
            pltpu.SMEM((micro,), jnp.int32),
            pltpu.VMEM((micro, rows, width), bf16),
            pltpu.VMEM((micro, rows, width), bf16),
            pltpu.VMEM((micro, rows, width), bf16),
            pltpu.VMEM((width, width), bf16),
            pltpu.VMEM((half, width), bf16),
            pltpu.VMEM((padded, width), f32),
            pltpu.VMEM((2, padded, half), bf16),
            pltpu.VMEM((2, padded, half), bf16),
            pltpu.VMEM((padded, half), bf16),
            pltpu.VMEM((padded, half), bf16),
            pltpu.VMEM((2, padded, half), bf16),
            pltpu.VMEM((2, padded, half), bf16),
            pltpu.VMEM((padded, half), bf16),
            pltpu.VMEM((padded, width), f32),
            pltpu.VMEM((3, n_dp, padded, half), bf16),
            pltpu.VMEM((2, n_dp, padded - lanes + share, lanes), bf16),
            pltpu.VMEM((2, n_dp, padded - lanes + share, lanes), bf16),
            pltpu.VMEM((share, half), f32),
            pltpu.VMEM((share, half), bf16),
            pltpu.VMEM((share, half), bf16),
            dma((6,)), dma((2,)), dma((2,)), dma((2,)), dma((2,)), dma((2,)), dma((2,)),
            dma((2,)), dma((2,)), dma((2, n_dp)), dma((2, n_dp)), dma((9, n_dp)), dma((3, n_dp)),
            dma((3, n_dp)), dma((3, n_dp)), dma, dma,
        ],
        compiler_params=pltpu.CompilerParams(
            collective_id=0, has_side_effects=True, vmem_limit_bytes=56 * 1024 * 1024
        ),
    )(batch_order, latents, control_hint, upstream, section_weight, zero_weight)
    grad_scale = 1.0 / math.sqrt(micro * rows * n_dp)
    return summed[None] * grad_scale


def solution(mesh):
    placed = (
        P(None, "dp", None),
        P(None, "dp", None),
        P(None, "dp", None),
        P(),
        P("section", None, None),
        P("section", None, None),
    )
    return jax.shard_map(
        functools.partial(body, mesh.shape["section"] // 2, mesh.shape["dp"]),
        mesh=mesh, in_specs=placed, out_specs=P("section", "dp", None), check_vma=False,
    )
```

```python
import functools
import math

import jax
import jax.numpy as jnp
from jax import lax
from jax.experimental import pallas as pl
from jax.experimental.pallas import tpu as pltpu
from jax.sharding import PartitionSpec as P

tanh_coef = 0.7978845608028654
cube_coef = 0.044715
f32 = jnp.float32
bf16 = jnp.bfloat16


def gelu_parts(values):
    square = values * values
    tangent = jnp.tanh(tanh_coef * (values + cube_coef * square * values))
    return square, tangent


def gelu_value(values):
    _, tangent = gelu_parts(values)
    return 0.5 * values * (1.0 + tangent)


def gelu_slope(values):
    square, tangent = gelu_parts(values)
    return 0.5 * (1.0 + tangent) + 0.5 * values * (1.0 - tangent * tangent) * tanh_coef * (
        1.0 + 3.0 * cube_coef * square
    )


def mm(left, right):
    return jnp.dot(left, right, preferred_element_type=f32)


def kernel(
    blocks, n_dp, order_any, lat_any, hint_any, up_any, w_any, z_any, out_ref,
    order, lat, hint, up, w, z, flat, chain, mine, side, hside, resid, pout, back, slope, gbuf,
    other, rside, et, ecol, acc, sent, ret, load_sem, chain_s, chain_r, side_s, side_r, resid_s, resid_r,
    back_s, back_r, e_s, e_r, ag_s, ag_r, sib_s, sib_r, ret_s, ret_r, rside_s, rside_r,
):
    sections = 2 * blocks
    line = n_dp // 2
    early = min(1, line - 1)
    micro, rows, width = lat.shape
    half = width // 2
    padded = flat.shape[0]
    share = ret.shape[0]
    lanes = et.shape[3]
    extra = padded - lanes
    place = lax.axis_index("section")
    me = lax.axis_index("dp")
    depth = place // 2
    parity = place % 2
    sibling = place + 1 - 2 * parity
    here, across = me // 2, me % 2
    partner = me + 1 - 2 * across
    is_base = parity == 0
    is_control = parity == 1
    first = depth == 0
    last = depth == blocks - 1
    aide = depth == blocks - 2
    active = (True, depth > 0, aide)
    cuts = [slice(0, half), slice(half, width)]

    when = pl.when
    loads = [
        (first, pltpu.make_async_copy(order_any, order, load_sem.at[0])),
        (first, pltpu.make_async_copy(lat_any, lat, load_sem.at[1])),
        (first & is_control, pltpu.make_async_copy(hint_any, hint, load_sem.at[2])),
        (depth >= blocks - 2, pltpu.make_async_copy(up_any, up, load_sem.at[3])),
    ]
    load_w = pltpu.make_async_copy(w_any.at[0], w, load_sem.at[4])
    load_z = pltpu.make_async_copy(z_any.at[0], z, load_sem.at[5])
    for needed, load in loads:

        @when(needed)
        def _():
            load.start()

    load_w.start()
    load_z.start()

    barrier = pltpu.get_barrier_semaphore()

    def greet(step, carry):
        pl.semaphore_signal(
            barrier, inc=1, device_id={"dp": lax.rem(me + step, n_dp)},
            device_id_type=pl.DeviceIdType.MESH,
        )
        return carry

    lax.fori_loop(1, n_dp, greet, 0)
    greeted = n_dp - 1
    for step in (-3, -2, -1, 1, 2, 3):
        there = place + step
        inside = (there >= 0) & (there < sections)

        @when(inside)
        def _():
            pl.semaphore_signal(
                barrier, inc=1, device_id={"section": there}, device_id_type=pl.DeviceIdType.MESH
            )

        greeted = greeted + jnp.where(inside, 1, 0)

    def remote(src, dst, send, recv, **where):
        return pltpu.make_async_remote_copy(
            src_ref=src, dst_ref=dst, send_sem=send, recv_sem=recv, device_id=where,
            device_id_type=pl.DeviceIdType.MESH,
        )

    for needed, load in loads:

        @when(needed)
        def _():
            load.wait()

    def fill(slot_rows, targets):
        flat[padded - 16 :, :] = jnp.zeros((16, width), f32)
        for slot in range(micro):
            flat[slot * rows : (slot + 1) * rows, :] = slot_rows(slot)
        for part in range(2):
            if targets[part] is not None:
                targets[part][...] = flat[:, cuts[part]].astype(bf16)

    @when(last)
    def _():
        fill(lambda slot: up[slot].astype(f32), [gbuf.at[0, me], other])

    @when(aide)
    def _():
        fill(lambda slot: up[slot].astype(f32), [None, gbuf.at[2, me]])

    def fill_first(slot_rows):
        fill(slot_rows, [chain.at[0], chain.at[1]])

    @when(first & is_base)
    def _():
        fill_first(lambda slot: lat[order[slot]].astype(f32))

    @when(first & is_control)
    def _():
        fill_first(lambda slot: lat[order[slot]].astype(f32) + hint[order[slot]].astype(f32))

    pl.semaphore_wait(barrier, greeted)

    def hop(stream, d, way, **where):
        return remote(
            gbuf.at[stream, d], gbuf.at[stream, d],
            ag_s.at[3 * stream + way, d], ag_r.at[stream, d], **where,
        )

    def go_up(stream, d):
        return hop(stream, d, 0, dp=me + 2)

    def go_down(stream, d):
        return hop(stream, d, 1, dp=me - 2)

    def go_across(stream, d):
        return hop(stream, d, 2, dp=partner)

    def go_sibling(stream, d):
        return remote(
            gbuf.at[stream, d], gbuf.at[stream, d], sib_s.at[stream, d], sib_r.at[stream, d], section=sibling
        )

    def gather_start(stream):
        @when(here + 1 < line)
        def _():
            go_up(stream, me).start()

        @when(here > 0)
        def _():
            go_down(stream, me).start()

        go_across(stream, me).start()

    def forward(stream, reach):
        @when(here - reach >= 0)
        def _():
            d = me - 2 * reach
            hop(stream, d, 2, dp=partner).wait_recv()

            @when(here + 1 < line)
            def _():
                go_up(stream, d).start()

            go_across(stream, d).start()
            go_sibling(stream, d).start()

        @when(here + reach < line)
        def _():
            d = me + 2 * reach
            hop(stream, d, 2, dp=partner).wait_recv()

            @when(here > 0)
            def _():
                go_down(stream, d).start()

            go_across(stream, d).start()
            go_sibling(stream, d).start()

    def sides(near, job):
        @when(here - near >= 0)
        def _():
            job(-2 * near)

        @when((here + near < line) & (near > 0))
        def _():
            job(2 * near)

    def cross(stream, near):
        def job(shift):
            d = partner + shift
            hop(stream, d, 2, dp=partner).wait_recv()
            go_sibling(stream, d).start()

        sides(near, job)

    def finish(stream, near):
        def job(shift):
            for d in (me + shift, partner + shift):
                if stream == 0:
                    given = is_base & ((d != me) | (first & jnp.logical_not(last)))
                elif stream == 1:
                    given = is_control
                else:
                    given = is_control & (d != me)

                @when(given)
                def _():
                    go_sibling(stream, d).wait_recv()

                @when(d != me)
                def _():
                    remote(
                        et.at[stream, d], ecol.at[stream, d], e_s.at[stream, 0],
                        e_r.at[stream, d], dp=partner,
                    ).wait_recv()

                term = mm(ecol[stream, d, extra:, :], gbuf[stream, d, :lanes, :])
                rest = ecol[stream, d, :extra, :].astype(f32).T[:share, :].astype(bf16)
                acc[stream] += term + mm(rest, gbuf[stream, d, lanes:, :])

        sides(near, job)

    def loop(low, high, step):
        def once(index, carry):
            step(index)
            return carry

        lax.fori_loop(low, high, once, 0)

    def gather_loop(stream):
        def step(reach):
            forward(stream, reach)
            cross(stream, reach - 1)
            finish(stream, reach - 1)

        loop(1, line + 1, step)

    def finish_loop(stream):
        loop(0, line, lambda near: finish(stream, near))

    @when(last & is_control)
    def _():
        gather_start(0)

    @when(aide & is_base)
    def _():
        gather_start(2)

    acc[...] = jnp.zeros_like(acc)
    et[...] = jnp.zeros_like(et)
    load_w.wait()

    def to_chain(part, target=None):
        target = place + 2 if target is None else target
        return remote(mine.at[part], chain.at[part], chain_s.at[part], chain_r.at[part], section=target)

    def to_side(target):
        return remote(mine.at[0], side, side_s.at[0], side_r.at[0], section=target)

    def to_hside(target):
        return remote(chain.at[0], hside, side_s.at[1], side_r.at[1], section=target)

    def to_resid(part, target):
        return remote(pout.at[part], resid.at[part], resid_s.at[part], resid_r.at[part], section=target)

    def to_back(target):
        return remote(back, gbuf.at[0, me], back_s.at[0], back_r.at[0], section=target)

    def to_earlier(target):
        return remote(gbuf.at[1, me], other, back_s.at[1], back_r.at[1], section=target)

    def to_aide(part, target):
        return remote(mine.at[part], rside, rside_s.at[part], rside_r, section=target)

    def to_return(stream, target):
        return remote(sent.at[stream - 1], ret, ret_s.at[stream - 1], ret_r, section=target)

    def give_back(stream, target):
        sent[stream - 1] = acc[stream].astype(bf16)
        to_return(stream, target).start()

    def spread(group, columns):
        wide = columns.astype(f32)
        turned = wide[:lanes, :].T
        for d in range(n_dp):
            mine_rows = slice(d * share, (d + 1) * share)
            et[group, d, :extra, :share] = wide[lanes:, mine_rows].astype(bf16)
            et[group, d, extra:, :] = turned[mine_rows, :].astype(bf16)
        ecol[group, me] = et[group, me]

        def send(step):
            there = lax.rem(me + step, n_dp)
            remote(
                et.at[group, there], ecol.at[group, me], e_s.at[group, step], e_r.at[group, me], dp=there
            ).start()

        loop(1, n_dp, send)

    @when(last & is_control)
    def _():
        for reach in range(1, early + 1):
            forward(0, reach)

    @when(is_control)
    def _():
        @when(depth > 0)
        def _():
            to_chain(0, sibling).wait_recv()
            to_hside(sibling).start()
            to_chain(1, sibling).wait_recv()

        for part in range(2):
            value = mm(chain[0], w[:half, cuts[part]]) + mm(chain[1], w[half:, cuts[part]])
            mine[part] = (chain[part].astype(f32) + gelu_value(value)).astype(bf16)
            if part == 0:
                to_side(place - 1).start()

            @when(jnp.logical_not(last))
            def _():
                to_chain(part).start()

            @when(last)
            def _():
                to_aide(part, place - 3 + part).start()

        load_z.wait()

        @when(jnp.logical_not(last))
        def _():
            for part in range(2):
                pout[part] = mm(mine[1], z[:, cuts[part]]).astype(bf16)
                to_resid(part, place - 1).start()

        @when(depth > 0)
        def _():
            spread(1, chain[1])

        spread(0, mine[1])

        @when(jnp.logical_not(last))
        def _():
            to_back(sibling).wait_recv()
            gather_start(0)
            go_sibling(0, me).start()

        @when(aide)
        def _():
            to_aide(1, sibling).wait_recv()
            spread(2, rside[...])
            finish_loop(2)
            give_back(2, place + 2)

        @when(jnp.logical_not(last))
        def _():
            gather_loop(0)

        @when(last)
        def _():
            loop(early + 1, line, lambda reach: forward(0, reach))
            loop(0, line, lambda near: cross(0, near))
            finish_loop(0)

        @when(depth > 0)
        def _():
            finish_loop(1)
            give_back(1, place - 2)

    @when(is_base)
    def _():
        @when(depth > 0)
        def _():
            to_hside(sibling).wait_recv()
            spread(1, hside[...])
            to_chain(0, sibling).wait_recv()

        slope[...] = mm(chain[0], w[:half, :])

        @when(last)
        def _():
            to_side(sibling).wait_recv()
            spread(0, side[...])

        @when(depth > 0)
        def _():
            to_chain(1, sibling).wait_recv()

        for part in range(2):
            value = slope[:, cuts[part]] + mm(chain[1], w[half:, cuts[part]])

            @when(depth > 0)
            def _():
                slope[:, cuts[part]] = gelu_slope(value)

            @when(jnp.logical_not(last))
            def _():
                flat[:, cuts[part]] = chain[part].astype(f32) + gelu_value(value)

        load_z.wait()

        @when(jnp.logical_not(last))
        def _():
            to_side(sibling).wait_recv()
            for part in range(2):
                flat[:, cuts[part]] += mm(side[...], z[:, cuts[part]])
            for part in range(2):
                to_resid(part, sibling).wait_recv()
                mine[part] = (flat[:, cuts[part]] + resid[part].astype(f32)).astype(bf16)
                to_chain(part).start()

        @when(first & jnp.logical_not(last))
        def _():
            spread(0, side[...])

        @when(aide)
        def _():
            loop(1, line, lambda reach: forward(2, reach))
            loop(0, line, lambda near: cross(2, near))
            to_aide(0, sibling).wait_recv()
            spread(2, rside[...])
            finish_loop(2)
            give_back(2, place + 2)

        @when(depth > 0)
        def _():
            @when(jnp.logical_not(last))
            def _():
                go_sibling(0, me).wait_recv()
                to_earlier(sibling).wait_recv()

            grads = [gbuf[0, me], other[...]]
            scaled = [
                (grads[part].astype(f32) * slope[:, cuts[part]]).astype(bf16) for part in range(2)
            ]
            for part in range(2):
                term = sum(
                    lax.dot_general(
                        scaled[inner], w[cuts[part], cuts[inner]], (((1,), (1,)), ((), ())),
                        preferred_element_type=f32,
                    )
                    for inner in range(2)
                )
                value = (grads[part].astype(f32) + term).astype(bf16)
                if part == 0:
                    back[...] = value
                    to_back(place - 1).start()
                else:
                    gbuf[1, me] = value
                    gather_start(1)
                    go_sibling(1, me).start()

                    @when(depth > 1)
                    def _():
                        to_earlier(place - 2).start()

        @when(depth > 0)
        def _():
            @when(jnp.logical_not(last))
            def _():
                spread(0, side[...])

            gather_loop(1)
            give_back(1, place - 2)

    @when(is_base)
    def _():
        finish_loop(0)

    @when(is_control)
    def _():
        to_side(place - 1).wait_send()

        @when(last)
        def _():
            for part in range(2):
                to_aide(part, place - 3 + part).wait_send()

        @when(depth > 0)
        def _():
            to_hside(sibling).wait_send()

        @when(jnp.logical_not(last))
        def _():
            for part in range(2):
                to_resid(part, place - 1).wait_send()

    @when(is_base & (depth > 0))
    def _():
        to_back(place - 1).wait_send()

        @when(depth > 1)
        def _():
            to_earlier(place - 2).wait_send()

    @when(jnp.logical_not(last))
    def _():
        for part in range(2):
            to_chain(part).wait_send()

    def drain(d):
        for stream in range(3):

            @when((is_control, is_base, is_base)[stream] & active[stream])
            def _():
                @when(d % 2 == across)
                def _():
                    @when((d <= me) & (here + 1 < line))
                    def _():
                        go_up(stream, d).wait_send()

                    @when((d >= me) & (here > 0))
                    def _():
                        go_down(stream, d).wait_send()

                    go_across(stream, d).wait_send()

                @when((d != me) | (jnp.logical_not(last), True, False)[stream])
                def _():
                    go_sibling(stream, d).wait_send()

            @when((d > 0) & active[stream])
            def _():
                remote(
                    et.at[stream, d], ecol.at[stream, d], e_s.at[stream, d], e_r.at[stream, d], dp=partner
                ).wait_send()

    loop(0, n_dp, drain)

    @when(depth > 0)
    def _():
        to_return(1, place - 2).wait_send()

    @when(aide)
    def _():
        to_return(2, place + 2).wait_send()

    to_return(1, sibling).wait_recv()
    out_ref[:, :half] = acc[0]
    out_ref[:, half:] = ret[...].astype(f32)


def body(blocks, n_dp, latents, control_hint, upstream, batch_order, section_weight, zero_weight):
    micro, rows, width = latents.shape
    half = zero_weight.shape[1]
    share = half // n_dp
    padded = (micro * rows + 15) // 16 * 16
    lanes = padded // 128 * 128
    vmem = pl.BlockSpec(memory_space=pltpu.VMEM)
    whole = pl.BlockSpec(memory_space=pl.ANY)
    dma = pltpu.SemaphoreType.DMA
    summed = pl.pallas_call(
        functools.partial(kernel, blocks, n_dp),
        out_shape=jax.ShapeDtypeStruct((share, width), f32),
        in_specs=[whole] * 6,
        out_specs=vmem,
        scratch_shapes=[
            pltpu.SMEM((micro,), jnp.int32),
            pltpu.VMEM((micro, rows, width), bf16),
            pltpu.VMEM((micro, rows, width), bf16),
            pltpu.VMEM((micro, rows, width), bf16),
            pltpu.VMEM((width, width), bf16),
            pltpu.VMEM((half, width), bf16),
            pltpu.VMEM((padded, width), f32),
            pltpu.VMEM((2, padded, half), bf16),
            pltpu.VMEM((2, padded, half), bf16),
            pltpu.VMEM((padded, half), bf16),
            pltpu.VMEM((padded, half), bf16),
            pltpu.VMEM((2, padded, half), bf16),
            pltpu.VMEM((2, padded, half), bf16),
            pltpu.VMEM((padded, half), bf16),
            pltpu.VMEM((padded, width), f32),
            pltpu.VMEM((3, n_dp, padded, half), bf16),
            pltpu.VMEM((padded, half), bf16),
            pltpu.VMEM((padded, half), bf16),
            pltpu.VMEM((3, n_dp, padded - lanes + share, lanes), bf16),
            pltpu.VMEM((3, n_dp, padded - lanes + share, lanes), bf16),
            pltpu.VMEM((3, share, half), f32),
            pltpu.VMEM((2, share, half), bf16),
            pltpu.VMEM((share, half), bf16),
            dma((6,)), dma((2,)), dma((2,)), dma((2,)), dma((2,)), dma((2,)), dma((2,)),
            dma((2,)), dma((2,)), dma((3, n_dp)), dma((3, n_dp)), dma((9, n_dp)), dma((3, n_dp)),
            dma((3, n_dp)), dma((3, n_dp)), dma((2,)), dma, dma((2,)), dma,
        ],
        compiler_params=pltpu.CompilerParams(
            collective_id=0, has_side_effects=True, vmem_limit_bytes=56 * 1024 * 1024
        ),
    )(batch_order, latents, control_hint, upstream, section_weight, zero_weight)
    grad_scale = 1.0 / math.sqrt(micro * rows * n_dp)
    return summed[None] * grad_scale


def solution(mesh):
    placed = (
        P(None, "dp", None),
        P(None, "dp", None),
        P(None, "dp", None),
        P(),
        P("section", None, None),
        P("section", None, None),
    )
    return jax.shard_map(
        functools.partial(body, mesh.shape["section"] // 2, mesh.shape["dp"]),
        mesh=mesh, in_specs=placed, out_specs=P("section", "dp", None), check_vma=False,
    )
```

```python
import functools
import math

import jax
import jax.numpy as jnp
from jax import lax
from jax.experimental import pallas as pl
from jax.experimental.pallas import tpu as pltpu
from jax.sharding import PartitionSpec as P

tanh_coef = 0.7978845608028654
cube_coef = 0.044715
f32 = jnp.float32
bf16 = jnp.bfloat16


def gelu_parts(values):
    square = values * values
    tangent = jnp.tanh(tanh_coef * (values + cube_coef * square * values))
    return square, tangent


def gelu_value(values):
    _, tangent = gelu_parts(values)
    return 0.5 * values * (1.0 + tangent)


def gelu_slope(values):
    square, tangent = gelu_parts(values)
    return 0.5 * (1.0 + tangent) + 0.5 * values * (1.0 - tangent * tangent) * tanh_coef * (
        1.0 + 3.0 * cube_coef * square
    )


def mm(left, right):
    return jnp.dot(left, right, preferred_element_type=f32)


def kernel(
    blocks, n_dp, grad_scale, order_any, lat_any, hint_any, up_any, w_any, z_any, out_ref,
    order, lat, hint, up, w, wt, z, flat, chain, mine, side, hside, resid, pout, back, slope, gbuf,
    other, rside, et, ecol, acc, sent, ret, load_sem, chain_s, chain_r, side_s, side_r, resid_s, resid_r,
    back_s, back_r, e_s, e_r, ag_s, ag_r, sib_s, sib_r, ret_s, ret_r, rside_s, rside_r,
):
    sections = 2 * blocks
    line = n_dp // 2
    early = min(1, line - 1)
    micro, rows, width = lat.shape
    half = width // 2
    padded = flat.shape[0]
    share = ret.shape[0]
    lanes = et.shape[3]
    extra = padded - lanes
    place = lax.axis_index("section")
    me = lax.axis_index("dp")
    depth = place // 2
    parity = place % 2
    sibling = place + 1 - 2 * parity
    here, across = me // 2, me % 2
    partner = me + 1 - 2 * across
    is_base = parity == 0
    is_control = parity == 1
    first = depth == 0
    last = depth == blocks - 1
    aide = depth == blocks - 2
    active = (True, depth > 0, aide)
    cuts = [slice(0, half), slice(half, width)]

    when = pl.when
    loads = [
        (first, pltpu.make_async_copy(order_any, order, load_sem.at[0])),
        (first, pltpu.make_async_copy(lat_any, lat, load_sem.at[1])),
        (first & is_control, pltpu.make_async_copy(hint_any, hint, load_sem.at[2])),
        (depth >= blocks - 2, pltpu.make_async_copy(up_any, up, load_sem.at[3])),
    ]
    load_w = pltpu.make_async_copy(w_any.at[0], w, load_sem.at[4])
    load_z = pltpu.make_async_copy(z_any.at[0], z, load_sem.at[5])
    for needed, load in loads:

        @when(needed)
        def _():
            load.start()

    load_w.start()
    load_z.start()

    barrier = pltpu.get_barrier_semaphore()

    def greet(step, carry):
        pl.semaphore_signal(
            barrier, inc=1, device_id={"dp": lax.rem(me + step, n_dp)},
            device_id_type=pl.DeviceIdType.MESH,
        )
        return carry

    lax.fori_loop(1, n_dp, greet, 0)
    greeted = n_dp - 1
    for step in (-3, -2, -1, 1, 2, 3):
        there = place + step
        inside = (there >= 0) & (there < sections)

        @when(inside)
        def _():
            pl.semaphore_signal(
                barrier, inc=1, device_id={"section": there}, device_id_type=pl.DeviceIdType.MESH
            )

        greeted = greeted + jnp.where(inside, 1, 0)

    def remote(src, dst, send, recv, **where):
        return pltpu.make_async_remote_copy(
            src_ref=src, dst_ref=dst, send_sem=send, recv_sem=recv, device_id=where,
            device_id_type=pl.DeviceIdType.MESH,
        )

    for needed, load in loads:

        @when(needed)
        def _():
            load.wait()

    def fill(slot_rows, targets):
        flat[padded - 16 :, :] = jnp.zeros((16, width), f32)
        for slot in range(micro):
            flat[slot * rows : (slot + 1) * rows, :] = slot_rows(slot)
        for part in range(2):
            if targets[part] is not None:
                targets[part][...] = flat[:, cuts[part]].astype(bf16)

    @when(last)
    def _():
        fill(lambda slot: up[slot].astype(f32), [gbuf.at[0, me], other])

    @when(aide)
    def _():
        fill(lambda slot: up[slot].astype(f32), [None, gbuf.at[2, me]])

    def fill_first(slot_rows):
        fill(slot_rows, [chain.at[0], chain.at[1]])

    @when(first & is_base)
    def _():
        fill_first(lambda slot: lat[order[slot]].astype(f32))

    @when(first & is_control)
    def _():
        fill_first(lambda slot: lat[order[slot]].astype(f32) + hint[order[slot]].astype(f32))

    pl.semaphore_wait(barrier, greeted)

    def hop(stream, d, way, **where):
        return remote(
            gbuf.at[stream, d], gbuf.at[stream, d],
            ag_s.at[3 * stream + way, d], ag_r.at[stream, d], **where,
        )

    def go_up(stream, d):
        return hop(stream, d, 0, dp=me + 2)

    def go_down(stream, d):
        return hop(stream, d, 1, dp=me - 2)

    def go_across(stream, d):
        return hop(stream, d, 2, dp=partner)

    def go_sibling(stream, d):
        return remote(
            gbuf.at[stream, d], gbuf.at[stream, d], sib_s.at[stream, d], sib_r.at[stream, d], section=sibling
        )

    def gather_start(stream):
        @when(here + 1 < line)
        def _():
            go_up(stream, me).start()

        @when(here > 0)
        def _():
            go_down(stream, me).start()

        go_across(stream, me).start()

    def forward(stream, reach):
        @when(here - reach >= 0)
        def _():
            d = me - 2 * reach
            hop(stream, d, 2, dp=partner).wait_recv()

            @when(here + 1 < line)
            def _():
                go_up(stream, d).start()

            go_across(stream, d).start()
            go_sibling(stream, d).start()

        @when(here + reach < line)
        def _():
            d = me + 2 * reach
            hop(stream, d, 2, dp=partner).wait_recv()

            @when(here > 0)
            def _():
                go_down(stream, d).start()

            go_across(stream, d).start()
            go_sibling(stream, d).start()

    def sides(near, job):
        @when(here - near >= 0)
        def _():
            job(-2 * near)

        @when((here + near < line) & (near > 0))
        def _():
            job(2 * near)

    def cross(stream, near):
        def job(shift):
            d = partner + shift
            hop(stream, d, 2, dp=partner).wait_recv()
            go_sibling(stream, d).start()

        sides(near, job)

    def finish(stream, near):
        def job(shift):
            for d in (me + shift, partner + shift):
                if stream == 0:
                    given = is_base & ((d != me) | (first & jnp.logical_not(last)))
                elif stream == 1:
                    given = is_control
                else:
                    given = is_control & (d != me)

                @when(given)
                def _():
                    go_sibling(stream, d).wait_recv()

                @when(d != me)
                def _():
                    remote(
                        et.at[stream, d], ecol.at[stream, d], e_s.at[stream, 0],
                        e_r.at[stream, d], dp=partner,
                    ).wait_recv()

                term = mm(ecol[stream, d, extra:, :], gbuf[stream, d, :lanes, :])
                rest = ecol[stream, d, :extra, :].astype(f32).T[:share, :].astype(bf16)
                acc[stream] += term + mm(rest, gbuf[stream, d, lanes:, :])

        sides(near, job)

    def loop(low, high, step):
        def once(index, carry):
            step(index)
            return carry

        lax.fori_loop(low, high, once, 0)

    def gather_loop(stream):
        def step(reach):
            forward(stream, reach)
            cross(stream, reach - 1)
            finish(stream, reach - 1)

        loop(1, line + 1, step)

    def finish_loop(stream):
        loop(0, line, lambda near: finish(stream, near))

    @when(last & is_control)
    def _():
        gather_start(0)

    @when(aide & is_base)
    def _():
        gather_start(2)

    acc[...] = jnp.zeros_like(acc)
    et[...] = jnp.zeros_like(et)
    load_w.wait()

    def to_chain(part, target=None):
        target = place + 2 if target is None else target
        return remote(mine.at[part], chain.at[part], chain_s.at[part], chain_r.at[part], section=target)

    def to_side(target):
        return remote(mine.at[0], side, side_s.at[0], side_r.at[0], section=target)

    def to_hside(target):
        return remote(chain.at[0], hside, side_s.at[1], side_r.at[1], section=target)

    def to_resid(part, target):
        return remote(pout.at[part], resid.at[part], resid_s.at[part], resid_r.at[part], section=target)

    def to_back(target):
        return remote(back, gbuf.at[0, me], back_s.at[0], back_r.at[0], section=target)

    def to_earlier(target):
        return remote(gbuf.at[1, me], other, back_s.at[1], back_r.at[1], section=target)

    def to_aide(part, target):
        return remote(mine.at[part], rside, rside_s.at[part], rside_r, section=target)

    def to_return(stream, target):
        return remote(sent.at[stream - 1], ret, ret_s.at[stream - 1], ret_r, section=target)

    def give_back(stream, target):
        sent[stream - 1] = acc[stream].astype(bf16)
        to_return(stream, target).start()

    def spread(group, columns):
        wide = columns.astype(f32)
        turned = wide[:lanes, :].T
        for d in range(n_dp):
            mine_rows = slice(d * share, (d + 1) * share)
            et[group, d, :extra, :share] = wide[lanes:, mine_rows].astype(bf16)
            et[group, d, extra:, :] = turned[mine_rows, :].astype(bf16)
        ecol[group, me] = et[group, me]

        def send(step):
            there = lax.rem(me + step, n_dp)
            remote(
                et.at[group, there], ecol.at[group, me], e_s.at[group, step], e_r.at[group, me], dp=there
            ).start()

        loop(1, n_dp, send)

    @when(last & is_control)
    def _():
        for reach in range(1, early + 1):
            forward(0, reach)

    @when(is_control)
    def _():
        @when(depth > 0)
        def _():
            to_chain(0, sibling).wait_recv()
            to_hside(sibling).start()
            to_chain(1, sibling).wait_recv()

        for part in range(2):
            value = mm(jnp.concatenate([chain[0], chain[1]], axis=1), w[:, cuts[part]])
            mine[part] = (chain[part].astype(f32) + gelu_value(value)).astype(bf16)
            if part == 0:
                to_side(place - 1).start()

            @when(jnp.logical_not(last))
            def _():
                to_chain(part).start()

            @when(last)
            def _():
                to_aide(part, place - 3 + part).start()

        load_z.wait()

        @when(jnp.logical_not(last))
        def _():
            for part in range(2):
                pout[part] = mm(mine[1], z[:, cuts[part]]).astype(bf16)
                to_resid(part, place - 1).start()

        @when(depth > 0)
        def _():
            spread(1, chain[1])

        spread(0, mine[1])

        @when(jnp.logical_not(last))
        def _():
            to_back(sibling).wait_recv()
            gather_start(0)
            go_sibling(0, me).start()

        @when(aide)
        def _():
            to_aide(1, sibling).wait_recv()
            spread(2, rside[...])
            finish_loop(2)
            give_back(2, place + 2)

        @when(jnp.logical_not(last))
        def _():
            gather_loop(0)

        @when(last)
        def _():
            loop(early + 1, line, lambda reach: forward(0, reach))
            loop(0, line, lambda near: cross(0, near))
            finish_loop(0)

        @when(depth > 0)
        def _():
            finish_loop(1)
            give_back(1, place - 2)

    @when(is_base)
    def _():
        @when(depth > 0)
        def _():
            block = 2 * 128
            for start in range(0, width, block):
                wt[:, start : start + block] = w[start : start + block, :].T
            to_hside(sibling).wait_recv()
            spread(1, hside[...])
            to_chain(0, sibling).wait_recv()

        slope[...] = mm(chain[0], w[:half, :])

        @when(last)
        def _():
            to_side(sibling).wait_recv()
            spread(0, side[...])

        @when(depth > 0)
        def _():
            to_chain(1, sibling).wait_recv()

        for part in range(2):
            value = slope[:, cuts[part]] + mm(chain[1], w[half:, cuts[part]])

            @when(depth > 0)
            def _():
                slope[:, cuts[part]] = gelu_slope(value)

            @when(jnp.logical_not(last))
            def _():
                flat[:, cuts[part]] = chain[part].astype(f32) + gelu_value(value)

        load_z.wait()

        @when(jnp.logical_not(last))
        def _():
            to_side(sibling).wait_recv()
            for part in range(2):
                flat[:, cuts[part]] += mm(side[...], z[:, cuts[part]])
            for part in range(2):
                to_resid(part, sibling).wait_recv()
                mine[part] = (flat[:, cuts[part]] + resid[part].astype(f32)).astype(bf16)
                to_chain(part).start()

        @when(first & jnp.logical_not(last))
        def _():
            spread(0, side[...])

        @when(aide)
        def _():
            loop(1, line, lambda reach: forward(2, reach))
            loop(0, line, lambda near: cross(2, near))
            to_aide(0, sibling).wait_recv()
            spread(2, rside[...])
            finish_loop(2)
            give_back(2, place + 2)

        @when(depth > 0)
        def _():
            @when(jnp.logical_not(last))
            def _():
                go_sibling(0, me).wait_recv()
                to_earlier(sibling).wait_recv()

            grads = [gbuf[0, me], other[...]]
            scaled = [
                (grads[part].astype(f32) * slope[:, cuts[part]]).astype(bf16) for part in range(2)
            ]
            for part in range(2):
                term = mm(jnp.concatenate(scaled, axis=1), wt[:, cuts[part]])
                value = (grads[part].astype(f32) + term).astype(bf16)
                if part == 0:
                    back[...] = value
                    to_back(place - 1).start()
                else:
                    gbuf[1, me] = value
                    gather_start(1)
                    go_sibling(1, me).start()

                    @when(depth > 1)
                    def _():
                        to_earlier(place - 2).start()

        @when(depth > 0)
        def _():
            @when(jnp.logical_not(last))
            def _():
                spread(0, side[...])

            gather_loop(1)
            give_back(1, place - 2)

    @when(is_base)
    def _():
        finish_loop(0)

    @when(is_control)
    def _():
        to_side(place - 1).wait_send()

        @when(last)
        def _():
            for part in range(2):
                to_aide(part, place - 3 + part).wait_send()

        @when(depth > 0)
        def _():
            to_hside(sibling).wait_send()

        @when(jnp.logical_not(last))
        def _():
            for part in range(2):
                to_resid(part, place - 1).wait_send()

    @when(is_base & (depth > 0))
    def _():
        to_back(place - 1).wait_send()

        @when(depth > 1)
        def _():
            to_earlier(place - 2).wait_send()

    @when(jnp.logical_not(last))
    def _():
        for part in range(2):
            to_chain(part).wait_send()

    def drain(d):
        for stream in range(3):

            @when((is_control, is_base, is_base)[stream] & active[stream])
            def _():
                @when(d % 2 == across)
                def _():
                    @when((d <= me) & (here + 1 < line))
                    def _():
                        go_up(stream, d).wait_send()

                    @when((d >= me) & (here > 0))
                    def _():
                        go_down(stream, d).wait_send()

                    go_across(stream, d).wait_send()

                @when((d != me) | (jnp.logical_not(last), True, False)[stream])
                def _():
                    go_sibling(stream, d).wait_send()

            @when((d > 0) & active[stream])
            def _():
                remote(
                    et.at[stream, d], ecol.at[stream, d], e_s.at[stream, d], e_r.at[stream, d], dp=partner
                ).wait_send()

    loop(0, n_dp, drain)

    @when(depth > 0)
    def _():
        to_return(1, place - 2).wait_send()

    @when(aide)
    def _():
        to_return(2, place + 2).wait_send()

    to_return(1, sibling).wait_recv()
    out_ref[0, :, :half] = acc[0] * grad_scale
    out_ref[0, :, half:] = ret[...].astype(f32) * grad_scale


def body(blocks, n_dp, latents, control_hint, upstream, batch_order, section_weight, zero_weight):
    micro, rows, width = latents.shape
    half = zero_weight.shape[1]
    share = half // n_dp
    padded = (micro * rows + 15) // 16 * 16
    lanes = padded // 128 * 128
    vmem = pl.BlockSpec(memory_space=pltpu.VMEM)
    whole = pl.BlockSpec(memory_space=pl.ANY)
    dma = pltpu.SemaphoreType.DMA
    grad_scale = 1.0 / math.sqrt(micro * rows * n_dp)
    return pl.pallas_call(
        functools.partial(kernel, blocks, n_dp, grad_scale),
        out_shape=jax.ShapeDtypeStruct((1, share, width), f32),
        in_specs=[whole] * 6,
        out_specs=vmem,
        scratch_shapes=[
            pltpu.SMEM((micro,), jnp.int32),
            pltpu.VMEM((micro, rows, width), bf16),
            pltpu.VMEM((micro, rows, width), bf16),
            pltpu.VMEM((micro, rows, width), bf16),
            pltpu.VMEM((width, width), bf16),
            pltpu.VMEM((width, width), bf16),
            pltpu.VMEM((half, width), bf16),
            pltpu.VMEM((padded, width), f32),
            pltpu.VMEM((2, padded, half), bf16),
            pltpu.VMEM((2, padded, half), bf16),
            pltpu.VMEM((padded, half), bf16),
            pltpu.VMEM((padded, half), bf16),
            pltpu.VMEM((2, padded, half), bf16),
            pltpu.VMEM((2, padded, half), bf16),
            pltpu.VMEM((padded, half), bf16),
            pltpu.VMEM((padded, width), f32),
            pltpu.VMEM((3, n_dp, padded, half), bf16),
            pltpu.VMEM((padded, half), bf16),
            pltpu.VMEM((padded, half), bf16),
            pltpu.VMEM((3, n_dp, padded - lanes + share, lanes), bf16),
            pltpu.VMEM((3, n_dp, padded - lanes + share, lanes), bf16),
            pltpu.VMEM((3, share, half), f32),
            pltpu.VMEM((2, share, half), bf16),
            pltpu.VMEM((share, half), bf16),
            dma((6,)), dma((2,)), dma((2,)), dma((2,)), dma((2,)), dma((2,)), dma((2,)),
            dma((2,)), dma((2,)), dma((3, n_dp)), dma((3, n_dp)), dma((9, n_dp)), dma((3, n_dp)),
            dma((3, n_dp)), dma((3, n_dp)), dma((2,)), dma, dma((2,)), dma,
        ],
        compiler_params=pltpu.CompilerParams(
            collective_id=0, has_side_effects=True, vmem_limit_bytes=56 * 1024 * 1024
        ),
    )(batch_order, latents, control_hint, upstream, section_weight, zero_weight)


def solution(mesh):
    placed = (
        P(None, "dp", None),
        P(None, "dp", None),
        P(None, "dp", None),
        P(),
        P("section", None, None),
        P("section", None, None),
    )
    return jax.shard_map(
        functools.partial(body, mesh.shape["section"] // 2, mesh.shape["dp"]),
        mesh=mesh, in_specs=placed, out_specs=P("section", "dp", None), check_vma=False,
    )
```

```python
import functools
import math

import jax
import jax.numpy as jnp
from jax import lax
from jax.experimental import pallas as pl
from jax.experimental.pallas import tpu as pltpu
from jax.sharding import PartitionSpec as P

tanh_coef = 0.7978845608028654
cube_coef = 0.044715
f32 = jnp.float32
bf16 = jnp.bfloat16


def gelu_parts(values):
    square = values * values
    tangent = jnp.tanh(tanh_coef * (values + cube_coef * square * values))
    return square, tangent


def gelu_value(values):
    _, tangent = gelu_parts(values)
    return 0.5 * values * (1.0 + tangent)


def gelu_slope(values):
    square, tangent = gelu_parts(values)
    return 0.5 * (1.0 + tangent) + 0.5 * values * (1.0 - tangent * tangent) * tanh_coef * (
        1.0 + 3.0 * cube_coef * square
    )


def mm(left, right):
    return jnp.dot(left, right, preferred_element_type=f32)


def kernel(
    blocks, n_dp, grad_scale, order_any, lat_any, hint_any, up_any, w_any, z_any, out_ref,
    order, lat, hint, up, w, wt, z, flat, chain, mine, side, hside, resid, pout, back, slope, gbuf,
    other, rside, et, ecol, acc, sent, ret, load_sem, chain_s, chain_r, side_s, side_r, resid_s, resid_r,
    back_s, back_r, e_s, e_r, ag_s, ag_r, sib_s, sib_r, ret_s, ret_r, rside_s, rside_r,
):
    sections = 2 * blocks
    line = n_dp // 2
    early = min(1, line - 1)
    micro, rows, width = lat.shape
    half = width // 2
    padded = flat.shape[0]
    share = ret.shape[0]
    lanes = et.shape[3]
    extra = padded - lanes
    place = lax.axis_index("section")
    me = lax.axis_index("dp")
    depth = place // 2
    parity = place % 2
    sibling = place + 1 - 2 * parity
    here, across = me // 2, me % 2
    partner = me + 1 - 2 * across
    is_base = parity == 0
    is_control = parity == 1
    first = depth == 0
    last = depth == blocks - 1
    aide = depth == blocks - 2
    active = (True, depth > 0, aide)
    cuts = [slice(0, half), slice(half, width)]
    quarter = half // 2
    pieces = [slice(0, quarter), slice(quarter, half)]

    when = pl.when
    loads = [
        (first, pltpu.make_async_copy(order_any, order, load_sem.at[0])),
        (first, pltpu.make_async_copy(lat_any, lat, load_sem.at[1])),
        (first & is_control, pltpu.make_async_copy(hint_any, hint, load_sem.at[2])),
        (depth >= blocks - 2, pltpu.make_async_copy(up_any, up, load_sem.at[3])),
    ]
    load_w = pltpu.make_async_copy(w_any.at[0], w, load_sem.at[4])
    load_z = pltpu.make_async_copy(z_any.at[0], z, load_sem.at[5])
    for needed, load in loads:

        @when(needed)
        def _():
            load.start()

    load_w.start()
    load_z.start()

    barrier = pltpu.get_barrier_semaphore()

    def greet(step, carry):
        pl.semaphore_signal(
            barrier, inc=1, device_id={"dp": lax.rem(me + step, n_dp)},
            device_id_type=pl.DeviceIdType.MESH,
        )
        return carry

    lax.fori_loop(1, n_dp, greet, 0)
    greeted = n_dp - 1
    for step in (-3, -2, -1, 1, 2, 3):
        there = place + step
        inside = (there >= 0) & (there < sections)

        @when(inside)
        def _():
            pl.semaphore_signal(
                barrier, inc=1, device_id={"section": there}, device_id_type=pl.DeviceIdType.MESH
            )

        greeted = greeted + jnp.where(inside, 1, 0)

    def remote(src, dst, send, recv, **where):
        return pltpu.make_async_remote_copy(
            src_ref=src, dst_ref=dst, send_sem=send, recv_sem=recv, device_id=where,
            device_id_type=pl.DeviceIdType.MESH,
        )

    for needed, load in loads:

        @when(needed)
        def _():
            load.wait()

    def fill(slot_rows, targets):
        flat[padded - 16 :, :] = jnp.zeros((16, width), f32)
        for slot in range(micro):
            flat[slot * rows : (slot + 1) * rows, :] = slot_rows(slot)
        for part in range(2):
            if targets[part] is not None:
                for piece in range(2):
                    span = slice(part * half + piece * quarter, part * half + (piece + 1) * quarter)
                    targets[part](piece)[...] = flat[:, span].astype(bf16)

    @when(last)
    def _():
        fill(lambda slot: up[slot].astype(f32), [lambda piece: gbuf.at[0, piece, me], lambda piece: other.at[piece]])

    @when(aide)
    def _():
        fill(lambda slot: up[slot].astype(f32), [None, lambda piece: gbuf.at[2, piece, me]])

    def fill_first(slot_rows):
        fill(slot_rows, [lambda piece: chain.at[0, :, pieces[piece]], lambda piece: chain.at[1, :, pieces[piece]]])

    @when(first & is_base)
    def _():
        fill_first(lambda slot: lat[order[slot]].astype(f32))

    @when(first & is_control)
    def _():
        fill_first(lambda slot: lat[order[slot]].astype(f32) + hint[order[slot]].astype(f32))

    pl.semaphore_wait(barrier, greeted)

    def hop(stream, piece, d, way, **where):
        return remote(
            gbuf.at[stream, piece, d], gbuf.at[stream, piece, d],
            ag_s.at[6 * stream + 2 * way + piece, d], ag_r.at[2 * stream + piece, d], **where,
        )

    def go_up(stream, piece, d):
        return hop(stream, piece, d, 0, dp=me + 2)

    def go_down(stream, piece, d):
        return hop(stream, piece, d, 1, dp=me - 2)

    def go_across(stream, piece, d):
        return hop(stream, piece, d, 2, dp=partner)

    def go_sibling(stream, piece, d):
        return remote(
            gbuf.at[stream, piece, d], gbuf.at[stream, piece, d],
            sib_s.at[2 * stream + piece, d], sib_r.at[2 * stream + piece, d], section=sibling,
        )

    def gather_start(stream, piece):
        @when(here + 1 < line)
        def _():
            go_up(stream, piece, me).start()

        @when(here > 0)
        def _():
            go_down(stream, piece, me).start()

        go_across(stream, piece, me).start()

    def forward(stream, reach):
        for piece in range(2):

            @when(here - reach >= 0)
            def _():
                d = me - 2 * reach
                go_across(stream, piece, d).wait_recv()

                @when(here + 1 < line)
                def _():
                    go_up(stream, piece, d).start()

                go_across(stream, piece, d).start()
                go_sibling(stream, piece, d).start()

            @when(here + reach < line)
            def _():
                d = me + 2 * reach
                go_across(stream, piece, d).wait_recv()

                @when(here > 0)
                def _():
                    go_down(stream, piece, d).start()

                go_across(stream, piece, d).start()
                go_sibling(stream, piece, d).start()

    def sides(near, job):
        @when(here - near >= 0)
        def _():
            job(-2 * near)

        @when((here + near < line) & (near > 0))
        def _():
            job(2 * near)

    def cross(stream, near):
        def job(shift):
            d = partner + shift
            for piece in range(2):
                go_across(stream, piece, d).wait_recv()
                go_sibling(stream, piece, d).start()

        sides(near, job)

    def finish(stream, near):
        def job(shift):
            for d in (me + shift, partner + shift):
                if stream == 0:
                    given = is_base & ((d != me) | (first & jnp.logical_not(last)))
                elif stream == 1:
                    given = is_control
                else:
                    given = is_control & (d != me)

                @when(given)
                def _():
                    for piece in range(2):
                        go_sibling(stream, piece, d).wait_recv()

                @when(d != me)
                def _():
                    remote(
                        et.at[stream, d], ecol.at[stream, d], e_s.at[stream, 0],
                        e_r.at[stream, d], dp=partner,
                    ).wait_recv()

                both = jnp.concatenate([gbuf[stream, 0, d], gbuf[stream, 1, d]], axis=1)
                term = mm(ecol[stream, d, extra:, :], both[:lanes, :])
                rest = ecol[stream, d, :extra, :].astype(f32).T[:share, :].astype(bf16)
                acc[stream] += term + mm(rest, both[lanes:, :])

        sides(near, job)

    def loop(low, high, step):
        def once(index, carry):
            step(index)
            return carry

        lax.fori_loop(low, high, once, 0)

    def gather_loop(stream):
        def step(reach):
            forward(stream, reach)
            cross(stream, reach - 1)
            finish(stream, reach - 1)

        loop(1, line + 1, step)

    def finish_loop(stream):
        loop(0, line, lambda near: finish(stream, near))

    @when(last & is_control)
    def _():
        for piece in range(2):
            gather_start(0, piece)

    @when(aide & is_base)
    def _():
        for piece in range(2):
            gather_start(2, piece)

    acc[...] = jnp.zeros_like(acc)
    et[...] = jnp.zeros_like(et)
    load_w.wait()

    def to_chain(part, target=None):
        target = place + 2 if target is None else target
        return remote(mine.at[part], chain.at[part], chain_s.at[part], chain_r.at[part], section=target)

    def to_side(target):
        return remote(mine.at[0], side, side_s.at[0], side_r.at[0], section=target)

    def to_hside(target):
        return remote(chain.at[0], hside, side_s.at[1], side_r.at[1], section=target)

    def to_resid(part, target):
        return remote(pout.at[part], resid.at[part], resid_s.at[part], resid_r.at[part], section=target)

    def to_back(piece, target):
        return remote(
            back.at[piece], gbuf.at[0, piece, me], back_s.at[piece], back_r.at[piece], section=target
        )

    def to_earlier(piece, target):
        return remote(
            gbuf.at[1, piece, me], other.at[piece], back_s.at[2 + piece], back_r.at[2 + piece], section=target
        )

    def to_aide(part, target):
        return remote(mine.at[part], rside, rside_s.at[part], rside_r, section=target)

    def to_return(stream, target):
        return remote(sent.at[stream - 1], ret, ret_s.at[stream - 1], ret_r, section=target)

    def give_back(stream, target):
        sent[stream - 1] = acc[stream].astype(bf16)
        to_return(stream, target).start()

    def spread(group, columns):
        wide = columns.astype(f32)
        turned = wide[:lanes, :].T
        for d in range(n_dp):
            mine_rows = slice(d * share, (d + 1) * share)
            et[group, d, :extra, :share] = wide[lanes:, mine_rows].astype(bf16)
            et[group, d, extra:, :] = turned[mine_rows, :].astype(bf16)
        ecol[group, me] = et[group, me]

        def send(step):
            there = lax.rem(me + step, n_dp)
            remote(
                et.at[group, there], ecol.at[group, me], e_s.at[group, step], e_r.at[group, me], dp=there
            ).start()

        loop(1, n_dp, send)

    @when(last & is_control)
    def _():
        for reach in range(1, early + 1):
            forward(0, reach)

    @when(is_control)
    def _():
        @when(depth > 0)
        def _():
            to_chain(0, sibling).wait_recv()
            to_hside(sibling).start()
            to_chain(1, sibling).wait_recv()

        for part in range(2):
            value = mm(jnp.concatenate([chain[0], chain[1]], axis=1), w[:, cuts[part]])
            mine[part] = (chain[part].astype(f32) + gelu_value(value)).astype(bf16)
            if part == 0:
                to_side(place - 1).start()

            @when(jnp.logical_not(last))
            def _():
                to_chain(part).start()

            @when(last)
            def _():
                to_aide(part, place - 3 + part).start()

        load_z.wait()

        @when(jnp.logical_not(last))
        def _():
            for part in range(2):
                pout[part] = mm(mine[1], z[:, cuts[part]]).astype(bf16)
                to_resid(part, place - 1).start()

        @when(depth > 0)
        def _():
            spread(1, chain[1])

        spread(0, mine[1])

        @when(jnp.logical_not(last))
        def _():
            @when(aide)
            def _():
                to_aide(1, sibling).wait_recv()
                spread(2, rside[...])

            for piece in range(2):
                to_back(piece, sibling).wait_recv()
                gather_start(0, piece)
                go_sibling(0, piece, me).start()

            forward(0, 1)

            @when(aide)
            def _():
                finish_loop(2)
                give_back(2, place + 2)

            cross(0, 0)
            finish(0, 0)

            def step(reach):
                forward(0, reach)
                cross(0, reach - 1)
                finish(0, reach - 1)

            loop(2, line + 1, step)

        @when(last)
        def _():
            loop(early + 1, line, lambda reach: forward(0, reach))
            loop(0, line, lambda near: cross(0, near))
            finish_loop(0)

        @when(depth > 0)
        def _():
            finish_loop(1)
            give_back(1, place - 2)

    @when(is_base)
    def _():
        @when(depth > 0)
        def _():
            block = 2 * 128
            for start in range(0, width, block):
                wt[:, start : start + block] = w[start : start + block, :].T
            to_hside(sibling).wait_recv()
            spread(1, hside[...])
            to_chain(0, sibling).wait_recv()

        slope[...] = mm(chain[0], w[:half, :])

        @when(last)
        def _():
            to_side(sibling).wait_recv()
            spread(0, side[...])

        @when(depth > 0)
        def _():
            to_chain(1, sibling).wait_recv()

        for part in range(2):
            value = slope[:, cuts[part]] + mm(chain[1], w[half:, cuts[part]])

            @when(depth > 0)
            def _():
                slope[:, cuts[part]] = gelu_slope(value)

            @when(jnp.logical_not(last))
            def _():
                flat[:, cuts[part]] = chain[part].astype(f32) + gelu_value(value)

        load_z.wait()

        @when(jnp.logical_not(last))
        def _():
            to_side(sibling).wait_recv()
            for part in range(2):
                flat[:, cuts[part]] += mm(side[...], z[:, cuts[part]])
            for part in range(2):
                to_resid(part, sibling).wait_recv()
                mine[part] = (flat[:, cuts[part]] + resid[part].astype(f32)).astype(bf16)
                to_chain(part).start()

        @when(first & jnp.logical_not(last))
        def _():
            spread(0, side[...])

        @when(aide)
        def _():
            loop(1, line, lambda reach: forward(2, reach))
            loop(0, line, lambda near: cross(2, near))
            to_aide(0, sibling).wait_recv()
            spread(2, rside[...])
            finish_loop(2)
            give_back(2, place + 2)

        @when(depth > 0)
        def _():
            @when(jnp.logical_not(last))
            def _():
                for piece in range(2):
                    go_sibling(0, piece, me).wait_recv()
                    to_earlier(piece, sibling).wait_recv()

            grads = [[gbuf[0, piece, me] for piece in range(2)], [other[piece] for piece in range(2)]]
            spans = [slice(index * quarter, (index + 1) * quarter) for index in range(4)]
            scaled = [
                (grads[index // 2][index % 2].astype(f32) * slope[:, spans[index]]).astype(bf16)
                for index in range(4)
            ]
            for index in range(4):
                part, piece = index // 2, index % 2
                term = mm(jnp.concatenate(scaled, axis=1), wt[:, spans[index]])
                value = (grads[part][piece].astype(f32) + term).astype(bf16)
                if part == 0:
                    back[piece] = value
                    to_back(piece, place - 1).start()
                else:
                    gbuf[1, piece, me] = value
                    gather_start(1, piece)
                    go_sibling(1, piece, me).start()

                    @when(depth > 1)
                    def _():
                        to_earlier(piece, place - 2).start()

        @when(depth > 0)
        def _():
            @when(jnp.logical_not(last))
            def _():
                spread(0, side[...])

            gather_loop(1)
            give_back(1, place - 2)

    @when(is_base)
    def _():
        finish_loop(0)

    @when(is_control)
    def _():
        to_side(place - 1).wait_send()

        @when(last)
        def _():
            for part in range(2):
                to_aide(part, place - 3 + part).wait_send()

        @when(depth > 0)
        def _():
            to_hside(sibling).wait_send()

        @when(jnp.logical_not(last))
        def _():
            for part in range(2):
                to_resid(part, place - 1).wait_send()

    @when(is_base & (depth > 0))
    def _():
        for piece in range(2):
            to_back(piece, place - 1).wait_send()

        @when(depth > 1)
        def _():
            for piece in range(2):
                to_earlier(piece, place - 2).wait_send()

    @when(jnp.logical_not(last))
    def _():
        for part in range(2):
            to_chain(part).wait_send()

    def drain(d):
        for stream in range(3):

            @when((is_control, is_base, is_base)[stream] & active[stream])
            def _():
                for piece in range(2):

                    @when(d % 2 == across)
                    def _():
                        @when((d <= me) & (here + 1 < line))
                        def _():
                            go_up(stream, piece, d).wait_send()

                        @when((d >= me) & (here > 0))
                        def _():
                            go_down(stream, piece, d).wait_send()

                        go_across(stream, piece, d).wait_send()

                    @when((d != me) | (jnp.logical_not(last), True, False)[stream])
                    def _():
                        go_sibling(stream, piece, d).wait_send()

            @when((d > 0) & active[stream])
            def _():
                remote(
                    et.at[stream, d], ecol.at[stream, d], e_s.at[stream, d], e_r.at[stream, d], dp=partner
                ).wait_send()

    loop(0, n_dp, drain)

    @when(depth > 0)
    def _():
        to_return(1, place - 2).wait_send()

    @when(aide)
    def _():
        to_return(2, place + 2).wait_send()

    to_return(1, sibling).wait_recv()
    out_ref[0, :, :half] = acc[0] * grad_scale
    out_ref[0, :, half:] = ret[...].astype(f32) * grad_scale


def body(blocks, n_dp, latents, control_hint, upstream, batch_order, section_weight, zero_weight):
    micro, rows, width = latents.shape
    half = zero_weight.shape[1]
    share = half // n_dp
    padded = (micro * rows + 15) // 16 * 16
    lanes = padded // 128 * 128
    vmem = pl.BlockSpec(memory_space=pltpu.VMEM)
    whole = pl.BlockSpec(memory_space=pl.ANY)
    dma = pltpu.SemaphoreType.DMA
    grad_scale = 1.0 / math.sqrt(micro * rows * n_dp)
    return pl.pallas_call(
        functools.partial(kernel, blocks, n_dp, grad_scale),
        out_shape=jax.ShapeDtypeStruct((1, share, width), f32),
        in_specs=[whole] * 6,
        out_specs=vmem,
        scratch_shapes=[
            pltpu.SMEM((micro,), jnp.int32),
            pltpu.VMEM((micro, rows, width), bf16),
            pltpu.VMEM((micro, rows, width), bf16),
            pltpu.VMEM((micro, rows, width), bf16),
            pltpu.VMEM((width, width), bf16),
            pltpu.VMEM((width, width), bf16),
            pltpu.VMEM((half, width), bf16),
            pltpu.VMEM((padded, width), f32),
            pltpu.VMEM((2, padded, half), bf16),
            pltpu.VMEM((2, padded, half), bf16),
            pltpu.VMEM((padded, half), bf16),
            pltpu.VMEM((padded, half), bf16),
            pltpu.VMEM((2, padded, half), bf16),
            pltpu.VMEM((2, padded, half), bf16),
            pltpu.VMEM((2, padded, half // 2), bf16),
            pltpu.VMEM((padded, width), f32),
            pltpu.VMEM((3, 2, n_dp, padded, half // 2), bf16),
            pltpu.VMEM((2, padded, half // 2), bf16),
            pltpu.VMEM((padded, half), bf16),
            pltpu.VMEM((3, n_dp, padded - lanes + share, lanes), bf16),
            pltpu.VMEM((3, n_dp, padded - lanes + share, lanes), bf16),
            pltpu.VMEM((3, share, half), f32),
            pltpu.VMEM((2, share, half), bf16),
            pltpu.VMEM((share, half), bf16),
            dma((6,)), dma((2,)), dma((2,)), dma((2,)), dma((2,)), dma((2,)), dma((2,)),
            dma((4,)), dma((4,)), dma((3, n_dp)), dma((3, n_dp)), dma((18, n_dp)), dma((6, n_dp)),
            dma((6, n_dp)), dma((6, n_dp)), dma((2,)), dma, dma((2,)), dma,
        ],
        compiler_params=pltpu.CompilerParams(
            collective_id=0, has_side_effects=True, vmem_limit_bytes=56 * 1024 * 1024
        ),
    )(batch_order, latents, control_hint, upstream, section_weight, zero_weight)


def solution(mesh):
    placed = (
        P(None, "dp", None),
        P(None, "dp", None),
        P(None, "dp", None),
        P(),
        P("section", None, None),
        P("section", None, None),
    )
    return jax.shard_map(
        functools.partial(body, mesh.shape["section"] // 2, mesh.shape["dp"]),
        mesh=mesh, in_specs=placed, out_specs=P("section", "dp", None), check_vma=False,
    )
```

```python
import functools
import math

import jax
import jax.numpy as jnp
from jax import lax
from jax.experimental import pallas as pl
from jax.experimental.pallas import tpu as pltpu
from jax.sharding import PartitionSpec as P

tanh_coef = 0.7978845608028654
cube_coef = 0.044715
f32 = jnp.float32
bf16 = jnp.bfloat16


def gelu_parts(values):
    square = values * values
    tangent = jnp.tanh(tanh_coef * (values + cube_coef * square * values))
    return square, tangent


def gelu_value(values):
    _, tangent = gelu_parts(values)
    return 0.5 * values * (1.0 + tangent)


def gelu_slope(values):
    square, tangent = gelu_parts(values)
    return 0.5 * (1.0 + tangent) + 0.5 * values * (1.0 - tangent * tangent) * tanh_coef * (
        1.0 + 3.0 * cube_coef * square
    )


def mm(left, right):
    return jnp.dot(left, right, preferred_element_type=f32)


def kernel(
    blocks, n_dp, grad_scale, order_any, lat_any, hint_any, up_any, w_any, z_any, out_ref,
    order, lat, hint, up, w, wt, z, flat, chain, mine, side, hside, resid, pout, back, slope, gbuf,
    other, rside, et, ecol, acc, sent, ret, load_sem, chain_s, chain_r, side_s, side_r, resid_s, resid_r,
    back_s, back_r, e_s, e_r, ag_s, ag_r, sib_s, sib_r, ret_s, ret_r, rside_s, rside_r,
):
    sections = 2 * blocks
    line = n_dp // 2
    early = min(1, line - 1)
    micro, rows, width = lat.shape
    half = width // 2
    padded = flat.shape[0]
    share = ret.shape[0]
    lanes = et.shape[3]
    extra = padded - lanes
    place = lax.axis_index("section")
    me = lax.axis_index("dp")
    depth = place // 2
    parity = place % 2
    sibling = place + 1 - 2 * parity
    here, across = me // 2, me % 2
    partner = me + 1 - 2 * across
    is_base = parity == 0
    is_control = parity == 1
    first = depth == 0
    last = depth == blocks - 1
    aide = depth == blocks - 2
    active = (True, depth > 0, aide)
    cuts = [slice(0, half), slice(half, width)]
    quarter = half // 2
    pieces = [slice(0, quarter), slice(quarter, half)]

    when = pl.when
    loads = [
        (first, pltpu.make_async_copy(order_any, order, load_sem.at[0])),
        (first, pltpu.make_async_copy(lat_any, lat, load_sem.at[1])),
        (first & is_control, pltpu.make_async_copy(hint_any, hint, load_sem.at[2])),
        (depth >= blocks - 2, pltpu.make_async_copy(up_any, up, load_sem.at[3])),
    ]
    load_w = pltpu.make_async_copy(w_any.at[0], w, load_sem.at[4])
    load_z = pltpu.make_async_copy(z_any.at[0], z, load_sem.at[5])
    for needed, load in loads:

        @when(needed)
        def _():
            load.start()

    load_w.start()
    load_z.start()

    barrier = pltpu.get_barrier_semaphore()

    def greet(step, carry):
        pl.semaphore_signal(
            barrier, inc=1, device_id={"dp": lax.rem(me + step, n_dp)},
            device_id_type=pl.DeviceIdType.MESH,
        )
        return carry

    lax.fori_loop(1, n_dp, greet, 0)
    greeted = n_dp - 1
    for step in (-3, -2, -1, 1, 2, 3):
        there = place + step
        inside = (there >= 0) & (there < sections)

        @when(inside)
        def _():
            pl.semaphore_signal(
                barrier, inc=1, device_id={"section": there}, device_id_type=pl.DeviceIdType.MESH
            )

        greeted = greeted + jnp.where(inside, 1, 0)

    def remote(src, dst, send, recv, **where):
        return pltpu.make_async_remote_copy(
            src_ref=src, dst_ref=dst, send_sem=send, recv_sem=recv, device_id=where,
            device_id_type=pl.DeviceIdType.MESH,
        )

    for needed, load in loads:

        @when(needed)
        def _():
            load.wait()

    def fill(slot_rows, targets):
        flat[padded - 16 :, :] = jnp.zeros((16, width), f32)
        for slot in range(micro):
            flat[slot * rows : (slot + 1) * rows, :] = slot_rows(slot)
        for part in range(2):
            if targets[part] is not None:
                for piece in range(2):
                    span = slice(part * half + piece * quarter, part * half + (piece + 1) * quarter)
                    targets[part](piece)[...] = flat[:, span].astype(bf16)

    @when(last)
    def _():
        fill(lambda slot: up[slot].astype(f32), [lambda piece: gbuf.at[0, piece, me], lambda piece: other.at[piece]])

    @when(aide)
    def _():
        fill(lambda slot: up[slot].astype(f32), [None, lambda piece: gbuf.at[2, piece, me]])

    def fill_first(slot_rows):
        fill(slot_rows, [lambda piece: chain.at[0, :, pieces[piece]], lambda piece: chain.at[1, :, pieces[piece]]])

    @when(first & is_base)
    def _():
        fill_first(lambda slot: lat[order[slot]].astype(f32))

    @when(first & is_control)
    def _():
        fill_first(lambda slot: lat[order[slot]].astype(f32) + hint[order[slot]].astype(f32))

    pl.semaphore_wait(barrier, greeted)

    def hop(stream, piece, d, way, **where):
        return remote(
            gbuf.at[stream, piece, d], gbuf.at[stream, piece, d],
            ag_s.at[6 * stream + 2 * way + piece, d], ag_r.at[2 * stream + piece, d], **where,
        )

    def go_up(stream, piece, d):
        return hop(stream, piece, d, 0, dp=me + 2)

    def go_down(stream, piece, d):
        return hop(stream, piece, d, 1, dp=me - 2)

    def go_across(stream, piece, d):
        return hop(stream, piece, d, 2, dp=partner)

    def go_sibling(stream, piece, d):
        return remote(
            gbuf.at[stream, piece, d], gbuf.at[stream, piece, d],
            sib_s.at[2 * stream + piece, d], sib_r.at[2 * stream + piece, d], section=sibling,
        )

    def gather_start(stream, piece):
        @when(here + 1 < line)
        def _():
            go_up(stream, piece, me).start()

        @when(here > 0)
        def _():
            go_down(stream, piece, me).start()

        go_across(stream, piece, me).start()

    def forward(stream, reach):
        for piece in range(2):

            @when(here - reach >= 0)
            def _():
                d = me - 2 * reach
                go_across(stream, piece, d).wait_recv()

                @when(here + 1 < line)
                def _():
                    go_up(stream, piece, d).start()

                go_across(stream, piece, d).start()
                go_sibling(stream, piece, d).start()

            @when(here + reach < line)
            def _():
                d = me + 2 * reach
                go_across(stream, piece, d).wait_recv()

                @when(here > 0)
                def _():
                    go_down(stream, piece, d).start()

                go_across(stream, piece, d).start()
                go_sibling(stream, piece, d).start()

    def sides(near, job):
        @when(here - near >= 0)
        def _():
            job(-2 * near)

        @when((here + near < line) & (near > 0))
        def _():
            job(2 * near)

    def cross(stream, near):
        def job(shift):
            d = partner + shift
            for piece in range(2):
                go_across(stream, piece, d).wait_recv()
                go_sibling(stream, piece, d).start()

        sides(near, job)

    def finish(stream, near):
        def job(shift):
            for d in (me + shift, partner + shift):
                if stream == 0:
                    given = is_base & ((d != me) | (first & jnp.logical_not(last)))
                elif stream == 1:
                    given = is_control
                else:
                    given = is_control & (d != me)

                @when(given)
                def _():
                    for piece in range(2):
                        go_sibling(stream, piece, d).wait_recv()

                @when(d != me)
                def _():
                    remote(
                        et.at[stream, d], ecol.at[stream, d], e_s.at[stream, 0],
                        e_r.at[stream, d], dp=partner,
                    ).wait_recv()

                both = jnp.concatenate([gbuf[stream, 0, d], gbuf[stream, 1, d]], axis=1)
                rest = ecol[stream, d, :extra, :].astype(f32).T[:share, :].astype(bf16)
                left = jnp.concatenate([ecol[stream, d, extra:, :], rest], axis=1)
                acc[stream] += mm(left, both)

        sides(near, job)

    def loop(low, high, step):
        def once(index, carry):
            step(index)
            return carry

        lax.fori_loop(low, high, once, 0)

    def gather_loop(stream):
        def step(reach):
            forward(stream, reach)
            cross(stream, reach - 1)
            finish(stream, reach - 1)

        loop(1, line + 1, step)

    def finish_loop(stream):
        loop(0, line, lambda near: finish(stream, near))

    @when(last & is_control)
    def _():
        for piece in range(2):
            gather_start(0, piece)

    @when(aide & is_base)
    def _():
        for piece in range(2):
            gather_start(2, piece)

    acc[...] = jnp.zeros_like(acc)
    et[...] = jnp.zeros_like(et)
    load_w.wait()

    def to_chain(part, target=None):
        target = place + 2 if target is None else target
        return remote(mine.at[part], chain.at[part], chain_s.at[part], chain_r.at[part], section=target)

    def to_side(target):
        return remote(mine.at[0], side, side_s.at[0], side_r.at[0], section=target)

    def to_hside(target):
        return remote(chain.at[0], hside, side_s.at[1], side_r.at[1], section=target)

    def to_resid(part, target):
        return remote(pout.at[part], resid.at[part], resid_s.at[part], resid_r.at[part], section=target)

    def to_back(piece, target):
        return remote(
            back.at[piece], gbuf.at[0, piece, me], back_s.at[piece], back_r.at[piece], section=target
        )

    def to_earlier(piece, target):
        return remote(
            gbuf.at[1, piece, me], other.at[piece], back_s.at[2 + piece], back_r.at[2 + piece], section=target
        )

    def to_aide(part, target):
        return remote(mine.at[part], rside, rside_s.at[part], rside_r, section=target)

    def to_return(stream, target):
        return remote(sent.at[stream - 1], ret, ret_s.at[stream - 1], ret_r, section=target)

    def give_back(stream, target):
        sent[stream - 1] = acc[stream].astype(bf16)
        to_return(stream, target).start()

    def spread(group, columns):
        wide = columns.astype(f32)
        turned = wide[:lanes, :].T
        for d in range(n_dp):
            mine_rows = slice(d * share, (d + 1) * share)
            et[group, d, :extra, :share] = wide[lanes:, mine_rows].astype(bf16)
            et[group, d, extra:, :] = turned[mine_rows, :].astype(bf16)
        ecol[group, me] = et[group, me]

        def send(step):
            there = lax.rem(me + step, n_dp)
            remote(
                et.at[group, there], ecol.at[group, me], e_s.at[group, step], e_r.at[group, me], dp=there
            ).start()

        loop(1, n_dp, send)

    @when(last & is_control)
    def _():
        for reach in range(1, early + 1):
            forward(0, reach)

    @when(is_control)
    def _():
        @when(depth > 0)
        def _():
            to_chain(0, sibling).wait_recv()
            to_hside(sibling).start()
            to_chain(1, sibling).wait_recv()

        for part in range(2):
            value = mm(jnp.concatenate([chain[0], chain[1]], axis=1), w[:, cuts[part]])
            mine[part] = (chain[part].astype(f32) + gelu_value(value)).astype(bf16)
            if part == 0:
                to_side(place - 1).start()

            @when(jnp.logical_not(last))
            def _():
                to_chain(part).start()

            @when(last)
            def _():
                to_aide(part, place - 3 + part).start()

        load_z.wait()

        @when(jnp.logical_not(last))
        def _():
            for part in range(2):
                pout[part] = mm(mine[1], z[:, cuts[part]]).astype(bf16)
                to_resid(part, place - 1).start()

        @when(depth > 0)
        def _():
            spread(1, chain[1])

        spread(0, mine[1])

        @when(jnp.logical_not(last))
        def _():
            @when(aide)
            def _():
                to_aide(1, sibling).wait_recv()
                spread(2, rside[...])

            for piece in range(2):
                to_back(piece, sibling).wait_recv()
                gather_start(0, piece)
                go_sibling(0, piece, me).start()

            forward(0, 1)

            @when(aide)
            def _():
                finish_loop(2)
                give_back(2, place + 2)

            cross(0, 0)
            finish(0, 0)

            def step(reach):
                forward(0, reach)
                cross(0, reach - 1)
                finish(0, reach - 1)

            loop(2, line + 1, step)

        @when(last)
        def _():
            loop(early + 1, line, lambda reach: forward(0, reach))
            loop(0, line, lambda near: cross(0, near))
            finish_loop(0)

        @when(depth > 0)
        def _():
            finish_loop(1)
            give_back(1, place - 2)

    @when(is_base)
    def _():
        @when(depth > 0)
        def _():
            block = 2 * 128
            for start in range(0, width, block):
                wt[:, start : start + block] = w[start : start + block, :].T
            to_hside(sibling).wait_recv()
            spread(1, hside[...])
            to_chain(0, sibling).wait_recv()

        slope[...] = mm(chain[0], w[:half, :])

        @when(last)
        def _():
            to_side(sibling).wait_recv()
            spread(0, side[...])

        @when(depth > 0)
        def _():
            to_chain(1, sibling).wait_recv()

        for part in range(2):
            value = slope[:, cuts[part]] + mm(chain[1], w[half:, cuts[part]])

            @when(depth > 0)
            def _():
                slope[:, cuts[part]] = gelu_slope(value)

            @when(jnp.logical_not(last))
            def _():
                flat[:, cuts[part]] = chain[part].astype(f32) + gelu_value(value)

        load_z.wait()

        @when(jnp.logical_not(last))
        def _():
            to_side(sibling).wait_recv()
            for part in range(2):
                flat[:, cuts[part]] += mm(side[...], z[:, cuts[part]])
            for part in range(2):
                to_resid(part, sibling).wait_recv()
                mine[part] = (flat[:, cuts[part]] + resid[part].astype(f32)).astype(bf16)
                to_chain(part).start()

        @when(first & jnp.logical_not(last))
        def _():
            spread(0, side[...])

        @when(aide)
        def _():
            loop(1, line, lambda reach: forward(2, reach))
            loop(0, line, lambda near: cross(2, near))
            to_aide(0, sibling).wait_recv()
            spread(2, rside[...])
            finish_loop(2)
            give_back(2, place + 2)

        @when(depth > 0)
        def _():
            @when(jnp.logical_not(last))
            def _():
                for piece in range(2):
                    go_sibling(0, piece, me).wait_recv()
                    to_earlier(piece, sibling).wait_recv()

            grads = [[gbuf[0, piece, me] for piece in range(2)], [other[piece] for piece in range(2)]]
            spans = [slice(index * quarter, (index + 1) * quarter) for index in range(4)]
            scaled = [
                (grads[index // 2][index % 2].astype(f32) * slope[:, spans[index]]).astype(bf16)
                for index in range(4)
            ]
            for index in range(4):
                part, piece = index // 2, index % 2
                term = mm(jnp.concatenate(scaled, axis=1), wt[:, spans[index]])
                value = (grads[part][piece].astype(f32) + term).astype(bf16)
                if part == 0:
                    back[piece] = value
                    to_back(piece, place - 1).start()
                else:
                    gbuf[1, piece, me] = value
                    gather_start(1, piece)
                    go_sibling(1, piece, me).start()

                    @when(depth > 1)
                    def _():
                        to_earlier(piece, place - 2).start()

        @when(depth > 0)
        def _():
            @when(jnp.logical_not(last))
            def _():
                spread(0, side[...])

            gather_loop(1)
            give_back(1, place - 2)

    @when(is_base)
    def _():
        finish_loop(0)

    @when(is_control)
    def _():
        to_side(place - 1).wait_send()

        @when(last)
        def _():
            for part in range(2):
                to_aide(part, place - 3 + part).wait_send()

        @when(depth > 0)
        def _():
            to_hside(sibling).wait_send()

        @when(jnp.logical_not(last))
        def _():
            for part in range(2):
                to_resid(part, place - 1).wait_send()

    @when(is_base & (depth > 0))
    def _():
        for piece in range(2):
            to_back(piece, place - 1).wait_send()

        @when(depth > 1)
        def _():
            for piece in range(2):
                to_earlier(piece, place - 2).wait_send()

    @when(jnp.logical_not(last))
    def _():
        for part in range(2):
            to_chain(part).wait_send()

    def drain(d):
        for stream in range(3):

            @when((is_control, is_base, is_base)[stream] & active[stream])
            def _():
                for piece in range(2):

                    @when(d % 2 == across)
                    def _():
                        @when((d <= me) & (here + 1 < line))
                        def _():
                            go_up(stream, piece, d).wait_send()

                        @when((d >= me) & (here > 0))
                        def _():
                            go_down(stream, piece, d).wait_send()

                        go_across(stream, piece, d).wait_send()

                    @when((d != me) | (jnp.logical_not(last), True, False)[stream])
                    def _():
                        go_sibling(stream, piece, d).wait_send()

            @when((d > 0) & active[stream])
            def _():
                remote(
                    et.at[stream, d], ecol.at[stream, d], e_s.at[stream, d], e_r.at[stream, d], dp=partner
                ).wait_send()

    loop(0, n_dp, drain)

    @when(depth > 0)
    def _():
        to_return(1, place - 2).wait_send()

    @when(aide)
    def _():
        to_return(2, place + 2).wait_send()

    to_return(1, sibling).wait_recv()
    out_ref[0, :, :half] = acc[0] * grad_scale
    out_ref[0, :, half:] = ret[...].astype(f32) * grad_scale


def body(blocks, n_dp, latents, control_hint, upstream, batch_order, section_weight, zero_weight):
    micro, rows, width = latents.shape
    half = zero_weight.shape[1]
    share = half // n_dp
    padded = (micro * rows + 15) // 16 * 16
    lanes = padded // 128 * 128
    vmem = pl.BlockSpec(memory_space=pltpu.VMEM)
    whole = pl.BlockSpec(memory_space=pl.ANY)
    dma = pltpu.SemaphoreType.DMA
    grad_scale = 1.0 / math.sqrt(micro * rows * n_dp)
    return pl.pallas_call(
        functools.partial(kernel, blocks, n_dp, grad_scale),
        out_shape=jax.ShapeDtypeStruct((1, share, width), f32),
        in_specs=[whole] * 6,
        out_specs=vmem,
        scratch_shapes=[
            pltpu.SMEM((micro,), jnp.int32),
            pltpu.VMEM((micro, rows, width), bf16),
            pltpu.VMEM((micro, rows, width), bf16),
            pltpu.VMEM((micro, rows, width), bf16),
            pltpu.VMEM((width, width), bf16),
            pltpu.VMEM((width, width), bf16),
            pltpu.VMEM((half, width), bf16),
            pltpu.VMEM((padded, width), f32),
            pltpu.VMEM((2, padded, half), bf16),
            pltpu.VMEM((2, padded, half), bf16),
            pltpu.VMEM((padded, half), bf16),
            pltpu.VMEM((padded, half), bf16),
            pltpu.VMEM((2, padded, half), bf16),
            pltpu.VMEM((2, padded, half), bf16),
            pltpu.VMEM((2, padded, half // 2), bf16),
            pltpu.VMEM((padded, width), f32),
            pltpu.VMEM((3, 2, n_dp, padded, half // 2), bf16),
            pltpu.VMEM((2, padded, half // 2), bf16),
            pltpu.VMEM((padded, half), bf16),
            pltpu.VMEM((3, n_dp, padded - lanes + share, lanes), bf16),
            pltpu.VMEM((3, n_dp, padded - lanes + share, lanes), bf16),
            pltpu.VMEM((3, share, half), f32),
            pltpu.VMEM((2, share, half), bf16),
            pltpu.VMEM((share, half), bf16),
            dma((6,)), dma((2,)), dma((2,)), dma((2,)), dma((2,)), dma((2,)), dma((2,)),
            dma((4,)), dma((4,)), dma((3, n_dp)), dma((3, n_dp)), dma((18, n_dp)), dma((6, n_dp)),
            dma((6, n_dp)), dma((6, n_dp)), dma((2,)), dma, dma((2,)), dma,
        ],
        compiler_params=pltpu.CompilerParams(
            collective_id=0, has_side_effects=True, vmem_limit_bytes=56 * 1024 * 1024
        ),
    )(batch_order, latents, control_hint, upstream, section_weight, zero_weight)


def solution(mesh):
    placed = (
        P(None, "dp", None),
        P(None, "dp", None),
        P(None, "dp", None),
        P(),
        P("section", None, None),
        P("section", None, None),
    )
    return jax.shard_map(
        functools.partial(body, mesh.shape["section"] // 2, mesh.shape["dp"]),
        mesh=mesh, in_specs=placed, out_specs=P("section", "dp", None), check_vma=False,
    )
```
